32 devices in a mesh: dp: 8 (over y, x, core), mp: 4 (over z).
Axes of the slice: x: 2, y: 2, z: 4, core: 2. Of those that a mesh axis runs over, the one named last changes fastest.
Arguments:
- tokens: bfloat16 [24, 256, 2048], P('dp'), may hold values from -6 to 6
- text: bfloat16 [24, 128, 2048], P('dp'), may hold values from -6 to 6
- text_len: int32 [24], P('dp'), may hold values from 5 to 128, as said below
- text_mask: int32 [24, 128], P('dp'), may hold values from 0 to 1, as said below
- cotangent: bfloat16 [24, 256, 2048], P('dp'), may hold values from -6 to 6
- w_self: bfloat16 [3, 2048, 2048], P(None, None, 'mp'), may hold values from -0.125 to 0.125
- wo_self: bfloat16 [2048, 2048], P('mp'), may hold values from -1 to 1
- wq_cross: bfloat16 [2048, 2048], P(None, 'mp'), may hold values from -0.125 to 0.125
- wkv_cross: bfloat16 [2, 2048, 2048], P(None, None, 'mp'), may hold values from -0.125 to 0.125
- wo_cross: bfloat16 [2048, 2048], P('mp'), may hold values from -0.75 to 0.75
- w_up: bfloat16 [2048, 8192], P(None, 'mp'), may hold values from -0.125 to 0.125
- bias_up: float32 [8192], P('mp'), may hold values from -3 to 3
- w_down: bfloat16 [8192, 2048], P('mp'), may hold values from -0.0625 to 0.0625
- bias_down: float32 [2048], replicated, may hold values from -3 to 3
- ln_gain: float32 [3, 2048], replicated, may hold values from 0.5 to 1.5
- ln_bias: float32 [3, 2048], replicated, may hold values from -3 to 3
Outputs:
- layer_out: bfloat16 [24, 256, 2048], P('dp')
- token_grad: float32 [24, 256, 2048], P('dp')
- text_grad: float32 [24, 128, 2048], P('dp')
- grad_w_self: float32 [3, 2048, 2048], P(None, 'dp', 'mp')
- grad_wo_self: float32 [2048, 2048], P('mp', 'dp')
- grad_wq_cross: float32 [2048, 2048], P('dp', 'mp')
- grad_wkv_cross: float32 [2, 2048, 2048], P(None, 'dp', 'mp')
- grad_wo_cross: float32 [2048, 2048], P('mp', 'dp')
- grad_w_up: float32 [2048, 8192], P('dp', 'mp')
- grad_bias_up: float32 [8192], P('mp')
- grad_w_down: float32 [8192, 2048], P('mp', 'dp')
- grad_bias_down: float32 [2048], replicated
- grad_ln_gain: float32 [3, 2048], replicated
- grad_ln_bias: float32 [3, 2048], replicated
The draws below stay inside these ranges and needn't reach their ends.
Inputs may be any that keep to these rules, and one draw needn't show every extreme that they name: `text_len`: every caption has at least 5 tokens and some caption fills all 128 slots. `text_mask`: the first caption slot of every image is kept.
All inputs are finite; a program needn't handle non-finite values.
Results may differ from the reference program's by a relative error of at most 0.03.
Values may be sent and summed in bfloat16 or wider, within the bound.
A program may use at most 256 MiB of HBM per device.

```python
import math
import jax
import jax.numpy as jnp
from jax import lax

D = 2048
HEADS = 16
HEAD_DIM = 128
FF = 8192
DT = 2048
SEQ = 256
LT = 128
BATCH = 24
N_MP = 4


def draw_text_len(key, part):
    key = jax.random.fold_in(key, 11)
    first_key, second_key = jax.random.split(key)
    lengths = jax.random.randint(first_key, (BATCH,), 5, LT + 1)
    order = jax.random.permutation(second_key, BATCH)
    lengths = lengths.at[order[0]].set(LT)
    lengths = lengths.at[order[1]].set(5)
    return lengths.astype(jnp.int32)


def draw_text_mask(key, part):
    key = jax.random.fold_in(key, 23)
    levels = jax.random.randint(key, (BATCH, LT), 0, 8)
    kept = jnp.where(levels != 0, 1, 0).astype(jnp.int32)
    kept = kept.at[:, 0].set(1)
    return kept


def spiked(drawn, key, source, target, blocks, factor):
    owner, partner = [(jnp.arange(drawn.shape[axis_at]) // (drawn.shape[axis_at] // blocks)).reshape([-1 if axis == axis_at else 1 for axis in range(drawn.ndim)]) for axis_at in (source, target)]
    chosen = jax.random.permutation(key, blocks)[partner]
    strong = (owner == chosen) | (owner == (partner + blocks // 2) % blocks)
    return jnp.where(strong, factor * drawn, drawn)


def block_levels(key, dims, cuts, smallest, high):
    loudness, own = 1.0, jax.random.fold_in(key, 6)
    for dim, shards_of in cuts:
        draws = jnp.exp(jax.random.uniform(jax.random.fold_in(own, dim), (shards_of,), jnp.float32, smallest / len(cuts), high / len(cuts)))
        loudness = loudness * jnp.repeat(draws, dims[dim] // shards_of).reshape([-1 if axis == dim else 1 for axis in range(len(dims))])
    return loudness


def gaussian(own_key, shape, deviation, limit, shards=(), held_as=jnp.bfloat16):
    level = block_levels(own_key, shape, shards, -0.22, 0.18) if shards else 1.0
    values = jax.random.normal(own_key, shape, jnp.float32) * deviation * level
    return jnp.minimum(jnp.maximum(values, -limit), limit).astype(held_as)


def gaussian_with(own_key, extent, spread, limit, cuts, heavy, kind=jnp.bfloat16):
    array = spread * jax.random.normal(own_key, extent, jnp.float32)
    if cuts:
        array = array * block_levels(own_key, extent, cuts, -0.22, 0.18)
    return jnp.clip(spiked(array, jax.random.fold_in(own_key, 3), *heavy), -limit, limit).astype(kind)


def setup_inputs(seed: int = 0) -> dict:
    seeds = jax.random.split(jax.random.key(seed), 17)
    return {
        "tokens": gaussian(seeds[0], (BATCH, SEQ, D), 1.0, 6.0, ((0, 8),)),
        "text": gaussian(seeds[1], (BATCH, LT, DT), 1.0, 6.0, ((0, 8),)),
        "text_len": draw_text_len(jax.random.fold_in(seeds[16], 71), 0),
        "text_mask": draw_text_mask(jax.random.fold_in(seeds[16], 71), 0),
        "cotangent": gaussian_with(seeds[4], (BATCH, SEQ, D), 1.0, 6.0, ((0, 8),), (0, 2, 8, 2.0)),
        "w_self": gaussian(seeds[5], (3, D, D), D ** -0.5, 0.125, ((2, 4),)),
        "wo_self": gaussian(seeds[6], (D, D), (D // 64) ** -0.5, 1.0, ((0, 4),)),
        "wq_cross": gaussian(seeds[7], (D, D), D ** -0.5, 0.125, ((1, 4),)),
        "wkv_cross": gaussian(seeds[8], (2, DT, D), DT ** -0.5, 0.125, ((2, 4),)),
        "wo_cross": gaussian(seeds[9], (D, D), (D // 32) ** -0.5, 0.75, ((0, 4),)),
        "w_up": gaussian(seeds[10], (D, FF), D ** -0.5, 0.125, ((1, 4),)),
        "bias_up": gaussian(seeds[11], (FF,), 0.5, 3.0, ((0, 4),), jnp.float32),
        "w_down": gaussian(seeds[12], (FF, D), FF ** -0.5, 0.0625, ((0, 4),)),
        "bias_down": gaussian(seeds[13], (D,), 0.5, 3.0, (), jnp.float32),
        "ln_gain": jnp.clip(1.0 + 0.1 * jax.random.normal(seeds[14], (3, D), jnp.float32), 0.5, 1.5),
        "ln_bias": gaussian(seeds[15], (3, D), 0.5, 3.0, (), jnp.float32),
    }


HIGHEST = lax.Precision.HIGHEST
MASKED = -1e+30
NORM_EPS = 1e-05

@jax.custom_vjp
def low(v):
    return lax.optimization_barrier(v.astype(jnp.bfloat16)).astype(jnp.float32)

@jax.custom_vjp
def low_back(v):
    return v

def low_keep(v):
    return (low(v), None)

def low_pass(kept, grad):
    return (grad,)

def back_keep(v):
    return (v, None)

def back_low(kept, grad):
    return (low(grad),)
low.defvjp(low_keep, low_pass)
low_back.defvjp(back_keep, back_low)

def gelu_exact(values):
    return 0.5 * values * (1.0 + lax.erf(values * 0.7071067811865476))

def layer_norm(hidden, norm_gain, norm_shift):
    row_mean = lax.optimization_barrier(jnp.mean(hidden, axis=-1, keepdims=True))
    centred = hidden - row_mean
    row_var = lax.optimization_barrier(jnp.mean(centred * centred, axis=-1, keepdims=True))
    return centred * lax.rsqrt(row_var + NORM_EPS) * norm_gain + norm_shift

def split_heads(values):
    return values.reshape(values.shape[0], values.shape[1], HEADS, HEAD_DIM)

def attention(queries, keys_in, values_in, key_valid):
    raw_scores = low_back(jnp.einsum('gqhe,gkhe->ghqk', queries, keys_in, precision=HIGHEST) * HEAD_DIM ** (-0.5))
    if key_valid is not None:
        raw_scores = jnp.where(key_valid[:, None, None, :], raw_scores, MASKED)
    row_max = lax.optimization_barrier(jnp.max(raw_scores, axis=-1, keepdims=True))
    exp_scores = jnp.exp(raw_scores - row_max)
    attn_prob = exp_scores / lax.optimization_barrier(jnp.sum(exp_scores, axis=-1, keepdims=True))
    mixed_heads = jnp.einsum('ghqk,gkhe->gqhe', low(attn_prob), values_in, precision=HIGHEST)
    mixed_heads = low_back(low(mixed_heads))
    return mixed_heads.reshape(mixed_heads.shape[0], mixed_heads.shape[1], HEADS * HEAD_DIM)

def branch_out(mixed_in, out_weight):
    groups, seq_len, inner_width = mixed_in.shape
    split_in = mixed_in.reshape(groups, seq_len, N_MP, inner_width // N_MP)
    split_weight = out_weight.reshape(N_MP, inner_width // N_MP, out_weight.shape[1])
    partial_out = jnp.einsum('gsnc,ncd->gsnd', split_in, split_weight, precision=HIGHEST)
    return lax.optimization_barrier(jnp.sum(low_back(low(partial_out)), axis=2))

def layer(hidden_in, text_in, key_valid, params):
    w_self, wo_self, wq_cross, wkv_cross, wo_cross, w_up, bias_up, w_down, bias_down, ln_gain, ln_bias = params
    normed_self = low(layer_norm(hidden_in, ln_gain[0], ln_bias[0]))
    projected = low_back(low(jnp.einsum('gsd,idc->igsc', normed_self, w_self, precision=HIGHEST)))
    mixed_self = attention(split_heads(projected[0]), split_heads(projected[1]), split_heads(projected[2]), None)
    after_self = hidden_in + branch_out(mixed_self, wo_self)
    normed_cross = low(layer_norm(after_self, ln_gain[1], ln_bias[1]))
    query_cross = low_back(low(jnp.einsum('gsd,dc->gsc', normed_cross, wq_cross, precision=HIGHEST)))
    text_low = low(text_in)
    key_value = low_back(low(jnp.einsum('gtd,idc->igtc', text_low, wkv_cross, precision=HIGHEST)))
    mixed_cross = attention(split_heads(query_cross), split_heads(key_value[0]), split_heads(key_value[1]), key_valid)
    after_cross = after_self + branch_out(mixed_cross, wo_cross)
    normed_mlp = low(layer_norm(after_cross, ln_gain[2], ln_bias[2]))
    pre_active = low_back(jnp.einsum('gsd,df->gsf', normed_mlp, w_up, precision=HIGHEST) + bias_up)
    active = low_back(low(gelu_exact(pre_active)))
    return after_cross + branch_out(active, w_down) + bias_down

def reference(tokens, text, text_len, text_mask, cotangent, w_self, wo_self, wq_cross, wkv_cross, wo_cross, w_up, bias_up, w_down, bias_down, ln_gain, ln_bias):
    position = jnp.arange(LT, dtype=jnp.int32)
    key_valid = (position[None, :] < text_len[:, None]) & (text_mask == 1)
    params = (w_self.astype(jnp.float32), wo_self.astype(jnp.float32), wq_cross.astype(jnp.float32), wkv_cross.astype(jnp.float32), wo_cross.astype(jnp.float32), w_up.astype(jnp.float32), bias_up.astype(jnp.float32), w_down.astype(jnp.float32), bias_down.astype(jnp.float32), ln_gain.astype(jnp.float32), ln_bias.astype(jnp.float32))
    group_size = math.gcd(BATCH, 16)
    group_count = BATCH // group_size

    def regroup(values):
        return values.reshape((group_count, group_size) + values.shape[1:])

    def whole(token_in, text_in, layer_params):

        def one_group(pieces):
            return layer(pieces[0], pieces[1], pieces[2], layer_params)
        result = lax.map(jax.checkpoint(one_group), (regroup(token_in), regroup(text_in), regroup(key_valid)))
        return result.reshape(token_in.shape)
    layer_sum, pullback = jax.vjp(whole, tokens.astype(jnp.float32), text.astype(jnp.float32), params)
    token_grad, text_grad, grads = pullback(cotangent.astype(jnp.float32))
    return (layer_sum.astype(jnp.bfloat16), token_grad, text_grad, grads[0], grads[1], grads[2], grads[3], grads[4], grads[5], grads[6], grads[7], grads[8], grads[9], grads[10])
```

```python
import functools
from typing import Any, NamedTuple

import jax
import jax.numpy as jnp
from jax import lax
from jax.experimental import pallas as pl
from jax.experimental.pallas import tpu as pltpu
from jax.sharding import PartitionSpec as P

HEAD_DIM = 128
MASKED = -1e30
NORM_EPS = 1e-05
PIECES = 4
STEP = 32
LOW = jnp.bfloat16
FULL = jnp.float32
MESH = pl.DeviceIdType.MESH
VMEM_LIMIT = 64 * 1024 * 1024 - 512 * 1024

class Inputs(NamedTuple):
    tokens: Any
    text: Any
    valid: Any
    cot: Any
    w_self: Any
    wo_self: Any
    wq: Any
    wkv: Any
    wo_cross: Any
    w_up: Any
    bias_up: Any
    w_down: Any
    bias_down: Any
    gain: Any
    shift: Any


class Outputs(NamedTuple):
    layer_out: Any
    token_grad: Any
    text_sum: Any
    shares: Any
    sums_out: Any
    norm1: Any
    norm2: Any
    norm3: Any
    low1: Any
    low2: Any
    act_all: Any
    pre_all: Any
    after_self: Any
    after_cross: Any
    grad_rows: Any
    staged: Any


class Scratch(NamedTuple):
    wide: Any
    down: Any
    kv_w: Any
    q_w: Any
    o_w: Any
    inbox: Any
    outbox: Any
    part: Any
    proj: Any
    mix1: Any
    prob1: Any
    q2: Any
    kv2: Any
    mix2: Any
    prob2: Any
    hid32: Any
    grad32: Any
    normed: Any
    rows16: Any
    d_pre: Any
    active: Any
    d_mix: Any
    tile: Any
    tile_sum: Any
    tile_in: Any
    unit_cols: Any
    x_text: Any
    sums: Any
    sums_in: Any
    send_sem: Any
    out_sem: Any
    in_sem: Any
    pass_sem: Any
    weight_sem: Any
    load_sem: Any
    store_sem: Any
    unit_sem: Any
    core_send: Any
    core_recv: Any
    chip_send: Any
    chip_recv: Any
    sum_send: Any
    sum_recv: Any


class Refs(NamedTuple):
    tokens: Any
    text: Any
    valid: Any
    cot: Any
    w_self: Any
    wo_self: Any
    wq: Any
    wkv: Any
    wo_cross: Any
    w_up: Any
    bias_up: Any
    w_down: Any
    bias_down: Any
    gain: Any
    shift: Any
    layer_out: Any
    token_grad: Any
    text_sum: Any
    shares: Any
    sums_out: Any
    norm1: Any
    norm2: Any
    norm3: Any
    low1: Any
    low2: Any
    act_all: Any
    pre_all: Any
    after_self: Any
    after_cross: Any
    grad_rows: Any
    staged: Any
    wide: Any
    down: Any
    kv_w: Any
    q_w: Any
    o_w: Any
    inbox: Any
    outbox: Any
    part: Any
    proj: Any
    mix1: Any
    prob1: Any
    q2: Any
    kv2: Any
    mix2: Any
    prob2: Any
    hid32: Any
    grad32: Any
    normed: Any
    rows16: Any
    d_pre: Any
    active: Any
    d_mix: Any
    tile: Any
    tile_sum: Any
    tile_in: Any
    unit_cols: Any
    x_text: Any
    sums: Any
    sums_in: Any
    send_sem: Any
    out_sem: Any
    in_sem: Any
    pass_sem: Any
    weight_sem: Any
    load_sem: Any
    store_sem: Any
    unit_sem: Any
    core_send: Any
    core_recv: Any
    chip_send: Any
    chip_recv: Any
    sum_send: Any
    sum_recv: Any


def dot_nn(left, right):
    return jnp.dot(left, right, preferred_element_type=FULL)


def dot_nt(left, right):
    return lax.dot_general(left, right, (((1,), (1,)), ((), ())), preferred_element_type=FULL)


def dot_tn(left, right):
    return lax.dot_general(left, right, (((0,), (0,)), ((), ())), preferred_element_type=FULL)


def mod(value, size):
    return value % size if isinstance(value, int) else lax.rem(value, size)


def at(index, size):
    return pl.ds(pl.multiple_of(index * size, size), size)


def loop(start, stop, body):
    def step(index, carry):
        body(index)
        return carry

    lax.fori_loop(start, stop, step, 0)


def layer_kernel(sizes, *refs):
    r = Refs(*refs)
    n_mp, n_dp, images, seq, width, text_rows, cols, hidden = sizes
    heads = cols // HEAD_DIM
    scale = HEAD_DIM**-0.5
    half = n_mp // 2
    slots = 2 * images
    piece = seq // PIECES
    small = text_rows // PIECES
    chips = n_dp // 2
    block = width // n_dp
    tile = min(512, hidden, width)
    wide, down, kv_w, q_w, o_w = r.wide, r.down, r.kv_w, r.q_w, r.o_w
    inbox, outbox, part = r.inbox, r.outbox, r.part
    hid32, grad32, normed, rows16 = r.hid32, r.grad32, r.normed, r.rows16
    proj, mix1, prob1, q2, kv2 = r.proj, r.mix1, r.prob1, r.q2, r.kv2
    mix2, prob2, d_pre, active, d_mix = r.mix2, r.prob2, r.d_pre, r.active, r.d_mix
    sums = r.sums
    place = lax.axis_index("mp")
    member = lax.axis_index("dp")
    core = lax.rem(member, 2)
    chip = lax.div(member, 2)
    low_half = place < half
    at_end = (place == 0) | (place == n_mp - 1)
    not_end = jnp.logical_not(at_end)
    at_mid = (place == half - 1) | (place == half)
    inner = jnp.where(low_half, place + 1, place - 1)
    outer = jnp.where(at_end, place, jnp.where(low_half, place - 1, place + 1))

    barrier = pltpu.get_barrier_semaphore()
    for hop in range(1, n_dp):
        pl.semaphore_signal(
            barrier, inc=1, device_id={"dp": lax.rem(member + hop, n_dp)}, device_id_type=MESH
        )
    pl.semaphore_signal(barrier, inc=1, device_id={"mp": inner}, device_id_type=MESH)
    if half > 1:

        @pl.when(not_end)
        def _():
            pl.semaphore_signal(barrier, inc=1, device_id={"mp": outer}, device_id_type=MESH)
            pl.semaphore_wait(barrier, n_dp + 1)

        @pl.when(at_end)
        def _():
            pl.semaphore_wait(barrier, n_dp)
    else:
        pl.semaphore_wait(barrier, n_dp)

    def load(src, dst, index):
        return pltpu.make_async_copy(src, dst, r.load_sem.at[index])

    def store(src, dst, index):
        return pltpu.make_async_copy(src, dst, r.store_sem.at[index])

    blocks = width // cols

    def self_weights():
        made = [
            pltpu.make_async_copy(
                r.w_self.at[j], wide.at[:, pl.ds(j * cols, cols)], r.weight_sem.at[j]
            )
            for j in range(3)
        ]
        for c in range(blocks):
            made.append(
                pltpu.make_async_copy(
                    r.wo_self.at[:, pl.ds(c * cols, cols)],
                    wide.at[pl.ds(c * cols, cols), pl.ds(3 * cols, cols)],
                    r.weight_sem.at[3 + c],
                )
            )
        return made

    other = 3 + blocks

    def up_weights():
        return [pltpu.make_async_copy(r.w_up, wide, r.weight_sem.at[0])]

    def down_weights():
        return [pltpu.make_async_copy(r.w_down, down, r.weight_sem.at[other])]

    def kv_weights():
        return [
            pltpu.make_async_copy(
                r.wkv.at[j], kv_w.at[:, pl.ds(j * cols, cols)], r.weight_sem.at[other + 1 + j]
            )
            for j in range(2)
        ]

    def cross_weights():
        return [
            pltpu.make_async_copy(r.wq, q_w, r.weight_sem.at[other + 3]),
            pltpu.make_async_copy(r.wo_cross, o_w, r.weight_sem.at[other + 4]),
        ]

    def start_all(copies):
        for copy in copies:
            copy.start()

    def wait_all(copies):
        for copy in copies:
            copy.wait()

    def wait_first(index, copies):
        @pl.when(index == 0)
        def _():
            wait_all(copies)

    def sum_copy(job, p, rows, swap):
        span = pl.ds(p * rows, rows)
        slot, deep = mod(job, images), mod(job, slots)
        return pltpu.make_async_remote_copy(
            src_ref=part.at[slot, span],
            dst_ref=inbox.at[deep, span] if swap else outbox.at[slot, span],
            send_sem=r.send_sem.at[slot, p],
            recv_sem=r.in_sem.at[deep, p] if swap else r.out_sem.at[slot, p],
            device_id={"mp": inner},
            device_id_type=MESH,
        )

    def pass_copy(job, p, rows):
        span = pl.ds(p * rows, rows)
        deep = mod(job, slots)
        return pltpu.make_async_remote_copy(
            src_ref=inbox.at[deep, span],
            dst_ref=inbox.at[deep, span],
            send_sem=r.pass_sem.at[deep, p],
            recv_sem=r.in_sem.at[deep, p],
            device_id={"mp": outer},
            device_id_type=MESH,
        )

    def emit(job, rows):
        @pl.when(at_end)
        def _():
            for p in range(PIECES):
                sum_copy(job, p, rows, half == 1).start()

    def fold(job, p, rows):
        if half == 1:
            return
        span = pl.ds(p * rows, rows)
        slot = mod(job, images)

        @pl.when(not_end)
        def _():
            sum_copy(job, p, rows, False).wait_recv()
            part[slot, span] = part[slot, span] + outbox[slot, span]

        @pl.when(at_mid)
        def _():
            sum_copy(job, p, rows, True).start()

        if half > 2:

            @pl.when(jnp.logical_not(at_mid | at_end))
            def _():
                sum_copy(job, p, rows, False).start()

    def spread(job, p, rows):
        span = pl.ds(p * rows, rows)
        slot, deep = mod(job, images), mod(job, slots)

        @pl.when(at_mid)
        def _():
            pass_copy(job, p, rows).wait_recv()
            inbox[deep, span] = part[slot, span] + inbox[deep, span]

        if half > 2:

            @pl.when(jnp.logical_not(at_mid | at_end))
            def _():
                pass_copy(job, p, rows).wait_recv()

        if half > 1:

            @pl.when(not_end)
            def _():
                pass_copy(job, p, rows).start()

    def settle(job, rows):
        for p in range(PIECES):
            sum_copy(job, p, rows, False).wait_send()
        if half > 1:

            @pl.when(not_end)
            def _():
                for p in range(PIECES):
                    pass_copy(job, p, rows).wait_send()

            @pl.when(at_end)
            def _():
                for p in range(PIECES):
                    pass_copy(job, p, rows).wait_recv()

    def service(job, rows, before, first=False, fill=(None, None)):
        def run(body):
            if first:
                pl.when(job > 0)(body)
            else:
                body()

        @run
        def _():
            fold(job - 1, 2, before)
            fold(job - 1, 3, before)
            spread(job - 1, 0, before)
            spread(job - 1, 1, before)

        if fill[0]:
            fill[0]()
        fold(job, 0, rows)

        @run
        def _():
            spread(job - 1, 2, before)

        if fill[1]:
            fill[1]()
        fold(job, 1, rows)

        @run
        def _():
            spread(job - 1, 3, before)

    def norm_stats(x):
        mean = jnp.mean(x, axis=-1, keepdims=True)
        centred = x - mean
        var = jnp.mean(centred * centred, axis=-1, keepdims=True)
        inv = lax.rsqrt(var + NORM_EPS)
        return centred * inv, inv

    def norm_forward(which, read, keep):
        def body(i):
            span = at(i, STEP)
            x = read(span)
            unit, _ = norm_stats(x)
            if keep:
                hid32[span, :] = x
            normed[span, :] = (
                unit * r.gain[which : which + 1, :] + r.shift[which : which + 1, :]
            ).astype(LOW)

        loop(0, seq // STEP, body)

    def norm_backward(which, read, deep, base, low):
        def body(i):
            span = at(i, STEP)
            unit, inv = norm_stats(read(span))
            grad = inbox[deep, span].astype(FULL)
            sums[which : which + 1, :] += jnp.sum(grad * unit, axis=0, keepdims=True)
            sums[3 + which : 4 + which, :] += jnp.sum(grad, axis=0, keepdims=True)
            scaled = grad * r.gain[which : which + 1, :]
            back = inv * (
                scaled
                - jnp.mean(scaled, axis=-1, keepdims=True)
                - unit * jnp.mean(scaled * unit, axis=-1, keepdims=True)
            )
            whole = base(span) + back
            grad32[span, :] = whole
            if low:
                normed[span, :] = whole.astype(LOW)

        loop(0, seq // STEP, body)

    def attend(queries, keys, values, valid):
        scores = dot_nt(queries, keys) * scale
        if valid is not None:
            scores = jnp.where(valid > 0.5, scores, MASKED)
        powers = jnp.exp(scores - jnp.max(scores, axis=-1, keepdims=True))
        weight = (powers / jnp.sum(powers, axis=-1, keepdims=True)).astype(LOW)
        return dot_nn(weight, values).astype(LOW), weight

    def attend_back(d_out, queries, keys, values, weight):
        prob = weight.astype(FULL)
        d_weight = dot_nt(d_out, values)
        d_value = dot_tn(weight, d_out)
        d_score = (
            prob * (d_weight - jnp.sum(d_weight * prob, axis=-1, keepdims=True))
        ).astype(LOW)
        d_query = dot_nn(d_score, keys) * scale
        d_key = dot_tn(d_score, queries) * scale
        return d_query.astype(LOW), d_key.astype(LOW), d_value.astype(LOW)

    def head(h, group=0):
        return pl.ds(group * cols + h * HEAD_DIM, HEAD_DIM)

    def chip_at(far):
        down_y = lax.rem(lax.div(chip, 2) + far // 2, chips // 2)
        return 2 * down_y + lax.rem(lax.rem(chip, 2) + far % 2, 2)

    def core_copy(turn):
        return pltpu.make_async_remote_copy(
            src_ref=r.tile.at[at(1 - core, block)],
            dst_ref=r.tile_in.at[mod(turn, 2)],
            send_sem=r.core_send.at[turn],
            recv_sem=r.core_recv.at[turn],
            device_id={"dp": member + 1 - 2 * core},
            device_id_type=MESH,
        )

    def chip_copy(turn, q, far):
        return pltpu.make_async_remote_copy(
            src_ref=r.staged.at[turn],
            dst_ref=r.shares.at[q, far],
            send_sem=r.chip_send.at[turn],
            recv_sem=r.chip_recv.at[q, far],
            device_id={"dp": 2 * chip_at(far) + core},
            device_id_type=MESH,
        )

    def unit_finish(turn):
        q, i = lax.div(turn, chips), lax.rem(turn, chips)
        slot = lax.rem(turn, 2)
        core_copy(turn).wait()

        def body(k):
            span = at(k, STEP)
            own = pl.ds(pl.multiple_of(core * block + k * STEP, STEP), STEP)
            r.tile_sum[span, :] = r.tile[own, :] + r.tile_in[slot, span]

        loop(0, block // STEP, body)

        @pl.when(i == chips - 1)
        def _():
            pltpu.make_async_copy(r.tile_sum, r.shares.at[q, 0], r.unit_sem.at[5]).start()

        @pl.when(i < chips - 1)
        def _():
            pltpu.make_async_copy(r.tile_sum, r.staged.at[turn], r.unit_sem.at[5]).start()

    def unit_send(turn):
        q, i = lax.div(turn, chips), lax.rem(turn, chips)
        pltpu.make_async_copy(r.tile_sum, r.staged.at[turn], r.unit_sem.at[5]).wait()

        @pl.when(i < chips - 1)
        def _():
            chip_copy(turn, q, i + 1).start()

    rows_all = images * seq
    text_all = images * text_rows

    def unit(q, i):
        turn = q * chips + i
        target = chip_at(mod(i + 1, chips))

        def x_load(which, src):
            return pltpu.make_async_copy(
                src.at[:, at(target, 2 * block)],
                r.x_text if which == 2 else r.unit_cols.at[which, :, pl.ds(0, 2 * block)],
                r.unit_sem.at[which],
            )

        def y_load(src, t):
            return pltpu.make_async_copy(
                src.at[:, pl.ds(t * tile, tile)],
                r.unit_cols.at[1 + t % 2, :, pl.ds(0, tile)],
                r.unit_sem.at[3 + t % 2],
            )

        def held(ref, rows, start):
            return ref[:, :, pl.ds(start, cols)].reshape(rows, cols)

        if q < 2:
            xs = [x_load(0, r.norm3 if q else r.cot)]
            ys = [y_load(r.pre_all if q else r.act_all, t) for t in range(hidden // tile)]
            start_all(ys[:2])
        elif q == 2:
            xs = [x_load(0, r.low2), x_load(1, r.norm2), x_load(2, r.text)]
        else:
            xs = [x_load(0, r.low1), x_load(1, r.norm1)]
        start_all(xs)

        @pl.when(turn > 0)
        def _():
            unit_finish(turn - 1)

        wait_all(xs)

        def turned(which):
            return r.unit_cols[which, :, : 2 * block].T

        def put(offset, left, right):
            r.tile[:, pl.ds(offset, right.shape[1])] = dot_nn(left, right).astype(LOW)

        if q < 2:
            left = turned(0)
            for t, copy in enumerate(ys):
                copy.wait()
                put(t * tile, left, r.unit_cols[1 + t % 2, :, :tile])
                if t + 2 < len(ys):
                    ys[t + 2].start()
        elif q == 2:
            put(0, turned(0), held(mix2, rows_all, 0))
            put(cols, turned(1), held(q2, rows_all, 0))
            left = r.x_text[...].T
            for j in range(2):
                put((2 + j) * cols, left, held(kv2, text_all, j * cols))
        else:
            put(0, turned(0), held(mix1, rows_all, 0))
            left = turned(1)
            for j in range(3):
                put((1 + j) * cols, left, held(proj, rows_all, j * cols))
        core_copy(turn).start()

        @pl.when(turn > 0)
        def _():
            unit_send(turn - 1)

    quarter = chips // 4

    def units(b, q):
        loop(b * quarter, (b + 1) * quarter, functools.partial(unit, q))

    start_all(self_weights())
    start_all(kv_weights())
    start_all(cross_weights())
    start_all(down_weights())
    sums[...] = jnp.zeros_like(sums)

    def image_rows(ref, b):
        return ref.at[at(b, seq)]

    def forward_self(b):
        get = load(image_rows(r.tokens, b), rows16, 0)
        get.start()
        get.wait()
        norm_forward(0, lambda span: rows16[span, :].astype(FULL), False)
        put = store(normed, image_rows(r.norm1, b), 0)
        put.start()
        wait_first(b, self_weights())

        def project(j):
            proj[b, :, at(j, cols)] = dot_nn(normed[...], wide[:, at(j, cols)]).astype(LOW)

        loop(0, 3, project)
        for h in range(heads):
            mixed, prob1[b, h] = attend(
                proj[b, :, head(h)], proj[b, :, head(h, 1)], proj[b, :, head(h, 2)], None
            )
            mix1[b, :, head(h)] = mixed

        def out(c):
            part[b, :, at(c, cols)] = dot_nn(
                mix1[b], wide[at(c, cols), pl.ds(3 * cols, cols)]
            ).astype(LOW)

        loop(0, blocks, out)
        emit(b, piece)
        get = load(r.text.at[at(b, text_rows)], rows16.at[pl.ds(0, text_rows)], 0)
        get.start()

        def text_side():
            get.wait()
            wait_first(b, kv_weights())

            def key_value(j):
                kv2[b, :, at(j, cols)] = dot_nn(
                    rows16[pl.ds(0, text_rows), :], kv_w[:, at(j, cols)]
                ).astype(LOW)

            loop(0, 2, key_value)

        service(b, piece, piece, first=True, fill=(text_side, None))
        put.wait()

    loop(0, images, forward_self)
    start_all(up_weights())

    def forward_cross(b):
        job = images + b
        get = load(image_rows(r.tokens, b), rows16, 0)
        get.start()
        settle(job - images, piece)
        get.wait()
        deep = mod(job - images, slots)
        norm_forward(
            1, lambda span: rows16[span, :].astype(FULL) + inbox[deep, span].astype(FULL), True
        )
        puts = [
            store(hid32, image_rows(r.after_self, b), 0),
            store(normed, image_rows(r.norm2, b), 1),
        ]
        start_all(puts)
        wait_first(b, cross_weights())
        q2[b] = dot_nn(normed[...], q_w[...]).astype(LOW)
        for h in range(heads):
            mixed, prob2[b, h] = attend(
                q2[b, :, head(h)], kv2[b, :, head(h)], kv2[b, :, head(h, 1)], r.valid[b]
            )
            mix2[b, :, head(h)] = mixed

        def out(t):
            part[b, :, at(t, tile)] = dot_nn(mix2[b], o_w[:, at(t, tile)]).astype(LOW)

        loop(0, width // tile, out)
        emit(job, piece)
        service(job, piece, piece)
        wait_all(puts)

    loop(0, images, forward_cross)

    def feed_forward(b):
        job = 2 * images + b
        gets = [
            load(image_rows(r.after_self, b), hid32, 0),
            load(image_rows(r.cot, b), rows16, 1),
        ]
        start_all(gets)
        settle(job - images, piece)
        wait_all(gets)
        deep = mod(job - images, slots)
        norm_forward(2, lambda span: hid32[span, :] + inbox[deep, span].astype(FULL), True)
        puts = [
            store(hid32, image_rows(r.after_cross, b), 0),
            store(normed, image_rows(r.norm3, b), 1),
        ]
        start_all(puts)
        wait_first(b, up_weights() + down_weights())

        def middle(t):
            span = at(t, tile)
            pre = dot_nn(normed[...], wide[:, span]) + r.bias_up[:, span]
            curve = 0.5 * (1.0 + lax.erf(pre * 0.7071067811865476))
            active[:, span] = (pre * curve).astype(LOW)
            slope = curve + pre * jnp.exp(-0.5 * pre * pre) * 0.3989422804014327
            d_active = dot_nt(rows16[...], down[span, :]).astype(LOW).astype(FULL)
            d_low = (d_active * slope).astype(LOW)
            d_pre[:, span] = d_low
            sums[7:8, span] += jnp.sum(d_low.astype(FULL), axis=0, keepdims=True)

        loop(0, hidden // tile, middle)
        more = [
            store(active, image_rows(r.act_all, b), 2),
            store(d_pre, image_rows(r.pre_all, b), 3),
        ]
        start_all(more)

        def back(t):
            part[b, :, at(t, tile)] = dot_nt(d_pre[...], wide[at(t, tile), :]).astype(LOW)

        loop(0, width // tile, back)
        emit(job, piece)
        service(job, piece, piece)
        wait_all(puts + more)

    loop(0, images, feed_forward)
    start_all(self_weights())

    def feed_out(job, b):
        get = load(image_rows(r.act_all, b), active, 0)
        get.start()
        settle(job - images, piece)
        get.wait()
        slot = mod(job, images)

        def out(t):
            part[slot, :, at(t, tile)] = dot_nn(active[...], down[:, at(t, tile)]).astype(LOW)

        loop(0, width // tile, out)
        emit(job, piece)

    def finish_out(job, b):
        get = load(image_rows(r.after_cross, b), hid32, 1)
        get.start()
        get.wait()
        deep = mod(job, slots)

        def body(i):
            span = at(i, STEP)
            rows16[span, :] = (
                hid32[span, :] + inbox[deep, span].astype(FULL) + r.bias_down[...]
            ).astype(LOW)

        loop(0, seq // STEP, body)
        put = store(rows16, image_rows(r.layer_out, b), 0)
        put.start()
        put.wait()

    feed_out(3 * images, 0)
    service(3 * images, piece, piece, fill=(lambda: units(0, 0), None))

    def backward_cross(b):
        job = 3 * images + 1 + b
        gets = [
            load(image_rows(r.after_cross, b), hid32, 0),
            load(image_rows(r.cot, b), rows16, 1),
        ]
        start_all(gets)
        settle(job - images, piece)
        wait_all(gets)

        def base(span):
            top = rows16[span, :].astype(FULL)
            sums[6:7, :] += jnp.sum(top, axis=0, keepdims=True)
            return top

        norm_backward(2, lambda span: hid32[span, :], mod(2 * images + b, slots), base, True)
        puts = [
            store(grad32, image_rows(r.grad_rows, b), 0),
            store(normed, image_rows(r.low2, b), 1),
        ]
        start_all(puts)
        d_mix[...] = dot_nt(normed[...], o_w[...]).astype(LOW)
        for h in range(heads):
            d_query, d_key, d_value = attend_back(
                d_mix[:, head(h)],
                q2[b, :, head(h)],
                kv2[b, :, head(h)],
                kv2[b, :, head(h, 1)],
                prob2[b, h],
            )
            q2[b, :, head(h)] = d_query
            kv2[b, :, head(h)] = d_key
            kv2[b, :, head(h, 1)] = d_value
        slot = mod(job, images)

        def out(t):
            part[slot, :, at(t, tile)] = dot_nt(q2[b], q_w[at(t, tile), :]).astype(LOW)

        loop(0, width // tile, out)
        emit(job, piece)
        service(job, piece, piece, fill=(lambda: units(1 + b, 0), None))
        wait_all(puts)

    loop(0, images, backward_cross)

    def second_out(b):
        job = 4 * images + b
        feed_out(job, b)

        @pl.when(b == 1)
        def _():
            finish_out(3 * images, 0)

        service(
            job,
            piece,
            piece,
            fill=(lambda: units(2 * b - 2, 1), lambda: units(2 * b - 1, 1)),
        )

    loop(1, images, second_out)

    def backward_self(b):
        job = 5 * images + b
        settle(job - images, piece)

        @pl.when(b > 0)
        def _():
            finish_out(4 * images + b, b)

        gets = [
            load(image_rows(r.after_self, b), hid32, 0),
            load(image_rows(r.grad_rows, b), grad32, 1),
        ]
        start_all(gets)
        wait_all(gets)
        norm_backward(
            1,
            lambda span: hid32[span, :],
            mod(3 * images + 1 + b, slots),
            lambda span: grad32[span, :],
            True,
        )
        puts = [
            store(grad32, image_rows(r.grad_rows, b), 0),
            store(normed, image_rows(r.low1, b), 1),
        ]
        start_all(puts)
        wait_first(b, self_weights())
        total = None
        for c in range(blocks):
            term = dot_nt(
                normed[:, pl.ds(c * cols, cols)], wide[pl.ds(c * cols, cols), pl.ds(3 * cols, cols)]
            )
            total = term if total is None else total + term
        d_mix[...] = total.astype(LOW)
        for h in range(heads):
            d_query, d_key, d_value = attend_back(
                d_mix[:, head(h)],
                proj[b, :, head(h)],
                proj[b, :, head(h, 1)],
                proj[b, :, head(h, 2)],
                prob1[b, h],
            )
            proj[b, :, head(h)] = d_query
            proj[b, :, head(h, 1)] = d_key
            proj[b, :, head(h, 2)] = d_value
        slot = mod(job, images)

        def out(t):
            part[slot, :, at(t, tile)] = dot_nt(
                proj[b], wide[at(t, tile), pl.ds(0, 3 * cols)]
            ).astype(LOW)

        loop(0, width // tile, out)
        emit(job, piece)
        service(
            job,
            piece,
            piece,
            fill=(lambda: units(b, 2), lambda: pl.when(b == images - 1)(lambda: units(3, 2))),
        )
        wait_all(puts)

    loop(0, images, backward_self)

    for b in range(images):
        job = 6 * images + b
        gets = [
            load(image_rows(r.tokens, b), rows16, 0),
            load(image_rows(r.grad_rows, b), grad32, 1),
        ]
        start_all(gets)
        settle(job - images, piece)
        slot = mod(job, images)

        def out(t, slot=slot, b=b):
            part[slot, :text_rows, at(t, tile)] = dot_nt(kv2[b], kv_w[at(t, tile), :]).astype(LOW)

        loop(0, width // tile, out)
        emit(job, small)
        wait_all(gets)
        norm_backward(
            0,
            lambda span: rows16[span, :].astype(FULL),
            mod(5 * images + b, slots),
            lambda span: grad32[span, :],
            False,
        )
        put = store(grad32, image_rows(r.token_grad, b), 0)
        put.start()
        late = [
            (lambda: units(0, 3), lambda: units(1, 3)),
            (lambda: units(2, 3), lambda: units(3, 3)),
            (lambda: unit_finish(4 * chips - 1), lambda: unit_send(4 * chips - 1)),
        ]
        service(job, small, piece if b == 0 else small, fill=late[b])
        put.wait()

    def small_copy(hop):
        return pltpu.make_async_remote_copy(
            src_ref=sums,
            dst_ref=r.sums_in.at[member],
            send_sem=r.sum_send.at[hop],
            recv_sem=r.sum_recv.at[hop],
            device_id={"dp": lax.rem(member + hop, n_dp)},
            device_id_type=MESH,
        )

    for hop in range(1, n_dp):
        small_copy(hop).start()
    r.sums_in[member] = sums[...]

    last = 7 * images - 1
    fold(last, 2, small)
    fold(last, 3, small)
    for p in range(PIECES):
        spread(last, p, small)
    for b in range(images):
        job = 6 * images + b
        settle(job, small)
        put = store(
            inbox.at[mod(job, slots), pl.ds(0, text_rows)],
            r.text_sum.at[at(b, text_rows)],
            b,
        )
        put.start()
        put.wait()

    for hop in range(1, n_dp):
        small_copy(hop).wait()
    whole = r.sums_in[0]
    for d in range(1, n_dp):
        whole = whole + r.sums_in[d]
    r.sums_out[...] = whole

    for q in range(4):
        for far in range(1, chips):
            chip_copy(q * chips + far - 1, q, far).wait()


class Ends(NamedTuple):
    layer_out: Any
    token_grad: Any
    text_grad: Any
    w_self: Any
    wo_self: Any
    wq: Any
    wkv: Any
    wo_cross: Any
    w_up: Any
    bias_up: Any
    w_down: Any
    bias_down: Any
    gain: Any
    shift: Any


class Held(NamedTuple):
    shares: Any
    text_low: Any
    text: Any
    token_grad: Any
    layer_out: Any
    w_self: Any
    wo_self: Any
    wq: Any
    wkv: Any
    wo_cross: Any
    w_up: Any
    w_down: Any
    load_sem: Any
    put_sem: Any


def closing_kernel(chips, cols, shares, token_grad, layer_out, text_sum, sums, *refs):
    ends = Ends(*refs[: len(Ends._fields)])
    held = Held(*refs[len(Ends._fields) :])
    parts = shares.shape[3] // cols
    text_load = pltpu.make_async_copy(text_sum, held.text_low, held.load_sem.at[4 * chips])
    loads = [
        [
            pltpu.make_async_copy(
                shares.at[q, c], held.shares.at[q, c], held.load_sem.at[q * chips + c]
            )
            for c in range(chips)
        ]
        for q in range(4)
    ]
    puts = []

    def put(src, dst):
        copy = pltpu.make_async_copy(src, dst, held.put_sem.at[len(puts)])
        copy.start()
        puts.append(copy)

    for q in range(4):
        for copy in loads[q]:
            copy.start()
    more = [
        pltpu.make_async_copy(token_grad, held.token_grad, held.load_sem.at[4 * chips + 1]),
        pltpu.make_async_copy(layer_out, held.layer_out, held.load_sem.at[4 * chips + 2]),
    ]
    for copy in more:
        copy.start()
    text_load.start()
    ends.bias_up[...] = sums[7:8, : ends.bias_up.shape[1]]
    ends.bias_down[...] = sums[6:7, :]
    ends.gain[...] = sums[0:3, :]
    ends.shift[...] = sums[3:6, :]

    def total(q, j):
        span = pl.ds(j * cols, cols)
        whole = held.shares[q, 0, :, span].astype(FULL)
        for c in range(1, chips):
            whole = whole + held.shares[q, c, :, span].astype(FULL)
        return whole

    for q in range(4):
        for copy in loads[q]:
            copy.wait()
        for j in range(parts):
            whole = total(q, j)
            if q == 0:
                held.w_down[pl.ds(j * cols, cols), :] = whole.T
            elif q == 1:
                held.w_up[:, pl.ds(j * cols, cols)] = whole
            elif j == 0:
                (held.wo_cross if q == 2 else held.wo_self)[...] = whole.T
            elif q == 3:
                held.w_self[j - 1] = whole
            elif j == 1:
                held.wq[...] = whole
            else:
                held.wkv[j - 2] = whole
        if q == 0:
            put(held.w_down, ends.w_down)
        elif q == 1:
            put(held.w_up, ends.w_up)
        elif q == 2:
            put(held.wo_cross, ends.wo_cross)
            put(held.wq, ends.wq)
            put(held.wkv, ends.wkv)
        else:
            put(held.wo_self, ends.wo_self)
            put(held.w_self, ends.w_self)
    more[0].wait()
    put(held.token_grad, ends.token_grad)
    more[1].wait()
    put(held.layer_out, ends.layer_out)
    text_load.wait()
    held.text[...] = held.text_low[...].astype(FULL)
    put(held.text, ends.text_grad)
    for copy in puts:
        copy.wait()


def local(
    n_mp,
    n_dp,
    tokens,
    text,
    text_len,
    text_mask,
    cotangent,
    w_self,
    wo_self,
    wq_cross,
    wkv_cross,
    wo_cross,
    w_up,
    bias_up,
    w_down,
    bias_down,
    ln_gain,
    ln_bias,
):
    images, seq, width = tokens.shape
    text_rows = text.shape[1]
    cols = w_self.shape[2]
    hidden = w_up.shape[1]
    heads = cols // HEAD_DIM
    rows = images * seq
    chips = n_dp // 2
    block = width // n_dp
    tile = min(512, hidden, width)
    position = lax.broadcasted_iota(jnp.int32, (images, text_rows), 1)
    valid = ((position < text_len[:, None]) & (text_mask == 1)).astype(FULL)

    def out(*shape, kind=LOW):
        return jax.ShapeDtypeStruct(shape, kind)

    outs = Outputs(
        layer_out=out(rows, width),
        token_grad=out(rows, width, kind=FULL),
        text_sum=out(images * text_rows, width),
        shares=out(4, chips, block, hidden),
        sums_out=out(8, width, kind=FULL),
        norm1=out(rows, width),
        norm2=out(rows, width),
        norm3=out(rows, width),
        low1=out(rows, width),
        low2=out(rows, width),
        act_all=out(rows, hidden),
        pre_all=out(rows, hidden),
        after_self=out(rows, width, kind=FULL),
        after_cross=out(rows, width, kind=FULL),
        grad_rows=out(rows, width, kind=FULL),
        staged=out(4 * chips, block, hidden),
    )
    slots = 2 * images

    def buf(*shape, kind=LOW):
        return pltpu.VMEM(shape, kind)

    dma = pltpu.SemaphoreType.DMA
    scratch = Scratch(
        wide=buf(width, hidden),
        down=buf(hidden, width),
        kv_w=buf(width, 2 * cols),
        q_w=buf(width, cols),
        o_w=buf(cols, width),
        inbox=buf(slots, seq, width),
        outbox=buf(images, seq, width),
        part=buf(images, seq, width),
        proj=buf(images, seq, 3 * cols),
        mix1=buf(images, seq, cols),
        prob1=buf(images, heads, seq, seq),
        q2=buf(images, seq, cols),
        kv2=buf(images, text_rows, 2 * cols),
        mix2=buf(images, seq, cols),
        prob2=buf(images, heads, seq, text_rows),
        hid32=buf(seq, width, kind=FULL),
        grad32=buf(seq, width, kind=FULL),
        normed=buf(seq, width),
        rows16=buf(seq, width),
        d_pre=buf(seq, hidden),
        active=buf(seq, hidden),
        d_mix=buf(seq, cols),
        tile=buf(2 * block, hidden),
        tile_sum=buf(block, hidden),
        tile_in=buf(2, block, hidden),
        unit_cols=buf(3, rows, max(tile, 2 * block)),
        x_text=buf(images * text_rows, 2 * block),
        sums=buf(8, width, kind=FULL),
        sums_in=buf(n_dp, 8, width, kind=FULL),
        send_sem=dma((images, PIECES)),
        out_sem=dma((images, PIECES)),
        in_sem=dma((slots, PIECES)),
        pass_sem=dma((slots, PIECES)),
        weight_sem=dma((3 + width // cols + 5,)),
        load_sem=dma((2,)),
        store_sem=dma((4,)),
        unit_sem=dma((6,)),
        core_send=dma((4 * chips,)),
        core_recv=dma((4 * chips,)),
        chip_send=dma((4 * chips,)),
        chip_recv=dma((4, chips)),
        sum_send=dma((n_dp,)),
        sum_recv=dma((n_dp,)),
    )
    vmem = pl.BlockSpec(memory_space=pltpu.VMEM)
    anywhere = pl.BlockSpec(memory_space=pl.ANY)
    sizes = (n_mp, n_dp, images, seq, width, text_rows, cols, hidden)
    results = pl.pallas_call(
        functools.partial(layer_kernel, sizes),
        out_shape=tuple(outs),
        in_specs=list(
            Inputs(*[anywhere] * len(Inputs._fields))._replace(
                valid=vmem, bias_up=vmem, bias_down=vmem, gain=vmem, shift=vmem
            )
        ),
        out_specs=tuple(Outputs(*[anywhere] * len(outs))._replace(sums_out=vmem)),
        scratch_shapes=list(scratch),
        compiler_params=pltpu.CompilerParams(
            collective_id=0, has_side_effects=True, vmem_limit_bytes=VMEM_LIMIT
        ),
        name="layer",
    )(
        tokens.reshape(rows, width),
        text.reshape(images * text_rows, width),
        valid.reshape(images, 1, text_rows),
        cotangent.reshape(rows, width),
        w_self,
        wo_self,
        wq_cross,
        wkv_cross,
        wo_cross,
        w_up,
        bias_up.reshape(1, hidden),
        w_down,
        bias_down.reshape(1, width),
        ln_gain,
        ln_bias,
    )
    got = Outputs(*results)
    shapes = Ends(
        layer_out=out(rows, width),
        token_grad=out(rows, width, kind=FULL),
        text_grad=out(images * text_rows, width, kind=FULL),
        w_self=out(3, block, cols, kind=FULL),
        wo_self=out(cols, block, kind=FULL),
        wq=out(block, cols, kind=FULL),
        wkv=out(2, block, cols, kind=FULL),
        wo_cross=out(cols, block, kind=FULL),
        w_up=out(block, hidden, kind=FULL),
        bias_up=out(1, hidden, kind=FULL),
        w_down=out(hidden, block, kind=FULL),
        bias_down=out(1, width, kind=FULL),
        gain=out(3, width, kind=FULL),
        shift=out(3, width, kind=FULL),
    )
    staging = Held(
        shares=buf(4, chips, block, hidden),
        text_low=buf(images * text_rows, width),
        text=buf(images * text_rows, width, kind=FULL),
        token_grad=buf(rows, width, kind=FULL),
        layer_out=buf(rows, width),
        w_self=buf(3, block, cols, kind=FULL),
        wo_self=buf(cols, block, kind=FULL),
        wq=buf(block, cols, kind=FULL),
        wkv=buf(2, block, cols, kind=FULL),
        wo_cross=buf(cols, block, kind=FULL),
        w_up=buf(block, hidden, kind=FULL),
        w_down=buf(hidden, block, kind=FULL),
        load_sem=dma((4 * chips + 3,)),
        put_sem=dma((10,)),
    )
    ends = Ends(
        *pl.pallas_call(
            functools.partial(closing_kernel, chips, cols),
            out_shape=tuple(shapes),
            in_specs=[anywhere] * 4 + [vmem],
            out_specs=tuple(
                Ends(*[anywhere] * len(shapes))._replace(
                    bias_up=vmem, bias_down=vmem, gain=vmem, shift=vmem
                )
            ),
            scratch_shapes=list(staging),
            compiler_params=pltpu.CompilerParams(vmem_limit_bytes=VMEM_LIMIT),
            name="closing",
        )(got.shares, got.token_grad, got.layer_out, got.text_sum, got.sums_out)
    )
    return (
        ends.layer_out.reshape(images, seq, width),
        ends.token_grad.reshape(images, seq, width),
        ends.text_grad.reshape(images, text_rows, width),
        ends.w_self,
        ends.wo_self,
        ends.wq,
        ends.wkv,
        ends.wo_cross,
        ends.w_up,
        ends.bias_up.reshape(hidden),
        ends.w_down,
        ends.bias_down.reshape(width),
        ends.gain,
        ends.shift,
    )


def solution(mesh):
    placed = (
        P("dp", None, None),
        P("dp", None, None),
        P("dp"),
        P("dp", None),
        P("dp", None, None),
        P(None, None, "mp"),
        P("mp", None),
        P(None, "mp"),
        P(None, None, "mp"),
        P("mp", None),
        P(None, "mp"),
        P("mp"),
        P("mp", None),
        P(),
        P(),
        P(),
    )
    return jax.shard_map(
        functools.partial(local, mesh.shape["mp"], mesh.shape["dp"]),
        mesh=mesh,
        in_specs=placed,
        out_specs=(
            P("dp", None, None),
            P("dp", None, None),
            P("dp", None, None),
            P(None, "dp", "mp"),
            P("mp", "dp"),
            P("dp", "mp"),
            P(None, "dp", "mp"),
            P("mp", "dp"),
            P("dp", "mp"),
            P("mp"),
            P("mp", "dp"),
            P(),
            P(),
            P(),
        ),
        check_vma=False,
    )
```

```python
import functools
from typing import Any, NamedTuple

import jax
import jax.numpy as jnp
from jax import lax
from jax.experimental import pallas as pl
from jax.experimental.pallas import tpu as pltpu
from jax.sharding import PartitionSpec as P

HEAD_DIM = 128
MASKED = -1e30
NORM_EPS = 1e-05
PIECES = 4
STEP = 32
LOW = jnp.bfloat16
FULL = jnp.float32
MESH = pl.DeviceIdType.MESH
VMEM_LIMIT = 64 * 1024 * 1024 - 512 * 1024

class Inputs(NamedTuple):
    tokens: Any
    text: Any
    length: Any
    kept: Any
    cot: Any
    w_self: Any
    wo_self: Any
    wq: Any
    wkv: Any
    wo_cross: Any
    w_up: Any
    bias_up: Any
    w_down: Any
    bias_down: Any
    gain: Any
    shift: Any


class Outputs(NamedTuple):
    layer_out: Any
    token_grad: Any
    text_sum: Any
    shares: Any
    sums_out: Any
    norm1: Any
    norm2: Any
    norm3: Any
    low1: Any
    low2: Any
    act_all: Any
    pre_all: Any
    after_self: Any
    after_cross: Any
    grad_rows: Any
    staged: Any


class Scratch(NamedTuple):
    wide: Any
    down: Any
    kv_w: Any
    q_w: Any
    o_w: Any
    inbox: Any
    outbox: Any
    part: Any
    proj: Any
    mix1: Any
    prob1: Any
    q2: Any
    kv2: Any
    mix2: Any
    prob2: Any
    hid32: Any
    grad32: Any
    normed: Any
    rows16: Any
    d_pre: Any
    active: Any
    d_mix: Any
    tile: Any
    tile_sum: Any
    tile_in: Any
    unit_cols: Any
    x_text: Any
    sums: Any
    sums_in: Any
    send_sem: Any
    out_sem: Any
    in_sem: Any
    pass_sem: Any
    weight_sem: Any
    load_sem: Any
    store_sem: Any
    unit_sem: Any
    core_send: Any
    core_recv: Any
    chip_send: Any
    chip_recv: Any
    sum_send: Any
    sum_recv: Any


class Refs(NamedTuple):
    tokens: Any
    text: Any
    length: Any
    kept: Any
    cot: Any
    w_self: Any
    wo_self: Any
    wq: Any
    wkv: Any
    wo_cross: Any
    w_up: Any
    bias_up: Any
    w_down: Any
    bias_down: Any
    gain: Any
    shift: Any
    layer_out: Any
    token_grad: Any
    text_sum: Any
    shares: Any
    sums_out: Any
    norm1: Any
    norm2: Any
    norm3: Any
    low1: Any
    low2: Any
    act_all: Any
    pre_all: Any
    after_self: Any
    after_cross: Any
    grad_rows: Any
    staged: Any
    wide: Any
    down: Any
    kv_w: Any
    q_w: Any
    o_w: Any
    inbox: Any
    outbox: Any
    part: Any
    proj: Any
    mix1: Any
    prob1: Any
    q2: Any
    kv2: Any
    mix2: Any
    prob2: Any
    hid32: Any
    grad32: Any
    normed: Any
    rows16: Any
    d_pre: Any
    active: Any
    d_mix: Any
    tile: Any
    tile_sum: Any
    tile_in: Any
    unit_cols: Any
    x_text: Any
    sums: Any
    sums_in: Any
    send_sem: Any
    out_sem: Any
    in_sem: Any
    pass_sem: Any
    weight_sem: Any
    load_sem: Any
    store_sem: Any
    unit_sem: Any
    core_send: Any
    core_recv: Any
    chip_send: Any
    chip_recv: Any
    sum_send: Any
    sum_recv: Any


def dot_nn(left, right):
    return jnp.dot(left, right, preferred_element_type=FULL)


def dot_nt(left, right):
    return lax.dot_general(left, right, (((1,), (1,)), ((), ())), preferred_element_type=FULL)


def dot_tn(left, right):
    return lax.dot_general(left, right, (((0,), (0,)), ((), ())), preferred_element_type=FULL)


def mod(value, size):
    return value % size if isinstance(value, int) else lax.rem(value, size)


def at(index, size):
    return pl.ds(pl.multiple_of(index * size, size), size)


def loop(start, stop, body):
    def step(index, carry):
        body(index)
        return carry

    lax.fori_loop(start, stop, step, 0)


def layer_kernel(sizes, *refs):
    r = Refs(*refs)
    n_mp, n_dp, images, seq, width, text_rows, cols, hidden = sizes
    heads = cols // HEAD_DIM
    scale = HEAD_DIM**-0.5
    half = n_mp // 2
    slots = 2 * images
    piece = seq // PIECES
    small = text_rows // PIECES
    chips = n_dp // 2
    block = width // n_dp
    tile = min(512, hidden, width)
    wide, down, kv_w, q_w, o_w = r.wide, r.down, r.kv_w, r.q_w, r.o_w
    inbox, outbox, part = r.inbox, r.outbox, r.part
    hid32, grad32, normed, rows16 = r.hid32, r.grad32, r.normed, r.rows16
    proj, mix1, prob1, q2, kv2 = r.proj, r.mix1, r.prob1, r.q2, r.kv2
    mix2, prob2, d_pre, active, d_mix = r.mix2, r.prob2, r.d_pre, r.active, r.d_mix
    sums = r.sums
    place = lax.axis_index("mp")
    member = lax.axis_index("dp")
    core = lax.rem(member, 2)
    chip = lax.div(member, 2)
    low_half = place < half
    at_end = (place == 0) | (place == n_mp - 1)
    not_end = jnp.logical_not(at_end)
    at_mid = (place == half - 1) | (place == half)
    inner = jnp.where(low_half, place + 1, place - 1)
    outer = jnp.where(at_end, place, jnp.where(low_half, place - 1, place + 1))

    def load(src, dst, index):
        return pltpu.make_async_copy(src, dst, r.load_sem.at[index])

    def store(src, dst, index):
        return pltpu.make_async_copy(src, dst, r.store_sem.at[index])

    blocks = width // cols

    def self_weights():
        made = [
            pltpu.make_async_copy(
                r.w_self.at[j], wide.at[:, pl.ds(j * cols, cols)], r.weight_sem.at[j]
            )
            for j in range(3)
        ]
        for c in range(blocks):
            made.append(
                pltpu.make_async_copy(
                    r.wo_self.at[:, pl.ds(c * cols, cols)],
                    wide.at[pl.ds(c * cols, cols), pl.ds(3 * cols, cols)],
                    r.weight_sem.at[3 + c],
                )
            )
        return made

    other = 3 + blocks

    def up_weights():
        return [pltpu.make_async_copy(r.w_up, wide, r.weight_sem.at[0])]

    def down_weights():
        return [pltpu.make_async_copy(r.w_down, down, r.weight_sem.at[other])]

    def kv_weights():
        return [
            pltpu.make_async_copy(
                r.wkv.at[j], kv_w.at[:, pl.ds(j * cols, cols)], r.weight_sem.at[other + 1 + j]
            )
            for j in range(2)
        ]

    def cross_weights():
        return [
            pltpu.make_async_copy(r.wq, q_w, r.weight_sem.at[other + 3]),
            pltpu.make_async_copy(r.wo_cross, o_w, r.weight_sem.at[other + 4]),
        ]

    def start_all(copies):
        for copy in copies:
            copy.start()

    def wait_all(copies):
        for copy in copies:
            copy.wait()

    def wait_first(index, copies):
        @pl.when(index == 0)
        def _():
            wait_all(copies)

    def sum_copy(job, p, rows, swap):
        span = pl.ds(p * rows, rows)
        slot, deep = mod(job, images), mod(job, slots)
        return pltpu.make_async_remote_copy(
            src_ref=part.at[slot, span],
            dst_ref=inbox.at[deep, span] if swap else outbox.at[slot, span],
            send_sem=r.send_sem.at[slot, p],
            recv_sem=r.in_sem.at[deep, p] if swap else r.out_sem.at[slot, p],
            device_id={"mp": inner},
            device_id_type=MESH,
        )

    def pass_copy(job, p, rows):
        span = pl.ds(p * rows, rows)
        deep = mod(job, slots)
        return pltpu.make_async_remote_copy(
            src_ref=inbox.at[deep, span],
            dst_ref=inbox.at[deep, span],
            send_sem=r.pass_sem.at[deep, p],
            recv_sem=r.in_sem.at[deep, p],
            device_id={"mp": outer},
            device_id_type=MESH,
        )

    def emit(job, rows):
        @pl.when(at_end)
        def _():
            for p in range(PIECES):
                sum_copy(job, p, rows, half == 1).start()

    def fold(job, p, rows):
        if half == 1:
            return
        span = pl.ds(p * rows, rows)
        slot = mod(job, images)

        @pl.when(not_end)
        def _():
            sum_copy(job, p, rows, False).wait_recv()
            part[slot, span] = part[slot, span] + outbox[slot, span]

        @pl.when(at_mid)
        def _():
            sum_copy(job, p, rows, True).start()

        if half > 2:

            @pl.when(jnp.logical_not(at_mid | at_end))
            def _():
                sum_copy(job, p, rows, False).start()

    def spread(job, p, rows):
        span = pl.ds(p * rows, rows)
        slot, deep = mod(job, images), mod(job, slots)

        @pl.when(at_mid)
        def _():
            pass_copy(job, p, rows).wait_recv()
            inbox[deep, span] = part[slot, span] + inbox[deep, span]

        if half > 2:

            @pl.when(jnp.logical_not(at_mid | at_end))
            def _():
                pass_copy(job, p, rows).wait_recv()

        if half > 1:

            @pl.when(not_end)
            def _():
                pass_copy(job, p, rows).start()

    def settle(job, rows):
        for p in range(PIECES):
            sum_copy(job, p, rows, False).wait_send()
        if half > 1:

            @pl.when(not_end)
            def _():
                for p in range(PIECES):
                    pass_copy(job, p, rows).wait_send()

            @pl.when(at_end)
            def _():
                for p in range(PIECES):
                    pass_copy(job, p, rows).wait_recv()

    def service(job, rows, before, first=False, fill=(None, None)):
        def run(body):
            if first:
                pl.when(job > 0)(body)
            else:
                body()

        @run
        def _():
            fold(job - 1, 2, before)
            fold(job - 1, 3, before)
            spread(job - 1, 0, before)
            spread(job - 1, 1, before)

        if fill[0]:
            fill[0]()
        fold(job, 0, rows)

        @run
        def _():
            spread(job - 1, 2, before)

        if fill[1]:
            fill[1]()
        fold(job, 1, rows)

        @run
        def _():
            spread(job - 1, 3, before)

    def norm_stats(x):
        mean = jnp.mean(x, axis=-1, keepdims=True)
        centred = x - mean
        var = jnp.mean(centred * centred, axis=-1, keepdims=True)
        inv = lax.rsqrt(var + NORM_EPS)
        return centred * inv, inv

    def norm_forward(which, read, keep):
        def body(i):
            span = at(i, STEP)
            x = read(span)
            unit, _ = norm_stats(x)
            if keep:
                hid32[span, :] = x
            normed[span, :] = (
                unit * r.gain[which : which + 1, :] + r.shift[which : which + 1, :]
            ).astype(LOW)

        loop(0, seq // STEP, body)

    def norm_backward(which, read, deep, base, low):
        def body(i):
            span = at(i, STEP)
            unit, inv = norm_stats(read(span))
            grad = inbox[deep, span].astype(FULL)
            sums[which : which + 1, :] += jnp.sum(grad * unit, axis=0, keepdims=True)
            sums[3 + which : 4 + which, :] += jnp.sum(grad, axis=0, keepdims=True)
            scaled = grad * r.gain[which : which + 1, :]
            back = inv * (
                scaled
                - jnp.mean(scaled, axis=-1, keepdims=True)
                - unit * jnp.mean(scaled * unit, axis=-1, keepdims=True)
            )
            whole = base(span) + back
            grad32[span, :] = whole
            if low:
                normed[span, :] = whole.astype(LOW)

        loop(0, seq // STEP, body)

    def attend(queries, keys, values, valid):
        scores = dot_nt(queries, keys) * scale
        if valid is not None:
            scores = jnp.where(valid, scores, MASKED)
        powers = jnp.exp(scores - jnp.max(scores, axis=-1, keepdims=True))
        weight = (powers / jnp.sum(powers, axis=-1, keepdims=True)).astype(LOW)
        return dot_nn(weight, values).astype(LOW), weight

    def attend_back(d_out, queries, keys, values, weight):
        prob = weight.astype(FULL)
        d_weight = dot_nt(d_out, values)
        d_value = dot_tn(weight, d_out)
        d_score = (
            prob * (d_weight - jnp.sum(d_weight * prob, axis=-1, keepdims=True))
        ).astype(LOW)
        d_query = dot_nn(d_score, keys) * scale
        d_key = dot_tn(d_score, queries) * scale
        return d_query.astype(LOW), d_key.astype(LOW), d_value.astype(LOW)

    def head(h, group=0):
        return pl.ds(group * cols + h * HEAD_DIM, HEAD_DIM)

    def chip_at(far):
        down_y = lax.rem(lax.div(chip, 2) + far // 2, chips // 2)
        return 2 * down_y + lax.rem(lax.rem(chip, 2) + far % 2, 2)

    def core_copy(turn):
        return pltpu.make_async_remote_copy(
            src_ref=r.tile.at[at(1 - core, block)],
            dst_ref=r.tile_in.at[mod(turn, 2)],
            send_sem=r.core_send.at[turn],
            recv_sem=r.core_recv.at[turn],
            device_id={"dp": member + 1 - 2 * core},
            device_id_type=MESH,
        )

    def chip_copy(turn, q, far):
        return pltpu.make_async_remote_copy(
            src_ref=r.staged.at[turn],
            dst_ref=r.shares.at[q, far],
            send_sem=r.chip_send.at[turn],
            recv_sem=r.chip_recv.at[q, far],
            device_id={"dp": 2 * chip_at(far) + core},
            device_id_type=MESH,
        )

    def unit_finish(turn):
        q, i = lax.div(turn, chips), lax.rem(turn, chips)
        slot = lax.rem(turn, 2)
        core_copy(turn).wait()

        def body(k):
            span = at(k, STEP)
            own = pl.ds(pl.multiple_of(core * block + k * STEP, STEP), STEP)
            r.tile_sum[span, :] = r.tile[own, :] + r.tile_in[slot, span]

        loop(0, block // STEP, body)

        @pl.when(i == chips - 1)
        def _():
            pltpu.make_async_copy(r.tile_sum, r.shares.at[q, 0], r.unit_sem.at[5]).start()

        @pl.when(i < chips - 1)
        def _():
            pltpu.make_async_copy(r.tile_sum, r.staged.at[turn], r.unit_sem.at[5]).start()

    def unit_send(turn):
        q, i = lax.div(turn, chips), lax.rem(turn, chips)
        pltpu.make_async_copy(r.tile_sum, r.staged.at[turn], r.unit_sem.at[5]).wait()

        @pl.when(i < chips - 1)
        def _():
            chip_copy(turn, q, i + 1).start()

    rows_all = images * seq
    text_all = images * text_rows

    def unit(q, i):
        turn = q * chips + i
        target = chip_at(mod(i + 1, chips))

        def x_load(which, src):
            return pltpu.make_async_copy(
                src.at[:, at(target, 2 * block)],
                r.x_text if which == 2 else r.unit_cols.at[which, :, pl.ds(0, 2 * block)],
                r.unit_sem.at[which],
            )

        def y_load(src, t):
            return pltpu.make_async_copy(
                src.at[:, pl.ds(t * tile, tile)],
                r.unit_cols.at[1 + t % 2, :, pl.ds(0, tile)],
                r.unit_sem.at[3 + t % 2],
            )

        def held(ref, rows, start):
            return ref[:, :, pl.ds(start, cols)].reshape(rows, cols)

        if q < 2:
            xs = [x_load(0, r.norm3 if q else r.cot)]
            ys = [y_load(r.pre_all if q else r.act_all, t) for t in range(hidden // tile)]
            start_all(ys[:2])
        elif q == 2:
            xs = [x_load(0, r.low2), x_load(1, r.norm2), x_load(2, r.text)]
        else:
            xs = [x_load(0, r.low1), x_load(1, r.norm1)]
        start_all(xs)

        @pl.when(turn > 0)
        def _():
            unit_finish(turn - 1)

        wait_all(xs)

        def turned(which):
            return r.unit_cols[which, :, : 2 * block].T

        def put(offset, left, right):
            r.tile[:, pl.ds(offset, right.shape[1])] = dot_nn(left, right).astype(LOW)

        if q < 2:
            left = turned(0)
            for t, copy in enumerate(ys):
                copy.wait()
                put(t * tile, left, r.unit_cols[1 + t % 2, :, :tile])
                if t + 2 < len(ys):
                    ys[t + 2].start()
        elif q == 2:
            put(0, turned(0), held(mix2, rows_all, 0))
            put(cols, turned(1), held(q2, rows_all, 0))
            left = r.x_text[...].T
            for j in range(2):
                put((2 + j) * cols, left, held(kv2, text_all, j * cols))
        else:
            put(0, turned(0), held(mix1, rows_all, 0))
            left = turned(1)
            for j in range(3):
                put((1 + j) * cols, left, held(proj, rows_all, j * cols))
        core_copy(turn).start()

        @pl.when(turn > 0)
        def _():
            unit_send(turn - 1)

    quarter = chips // 4

    def units(b, q):
        loop(b * quarter, (b + 1) * quarter, functools.partial(unit, q))

    first_rows = load(r.tokens.at[pl.ds(0, seq)], rows16, 0)
    first_rows.start()
    start_all(self_weights())
    sums[...] = jnp.zeros_like(sums)

    barrier = pltpu.get_barrier_semaphore()
    for hop in range(1, n_dp):
        pl.semaphore_signal(
            barrier, inc=1, device_id={"dp": lax.rem(member + hop, n_dp)}, device_id_type=MESH
        )
    pl.semaphore_signal(barrier, inc=1, device_id={"mp": inner}, device_id_type=MESH)
    if half > 1:

        @pl.when(not_end)
        def _():
            pl.semaphore_signal(barrier, inc=1, device_id={"mp": outer}, device_id_type=MESH)
            pl.semaphore_wait(barrier, n_dp + 1)

        @pl.when(at_end)
        def _():
            pl.semaphore_wait(barrier, n_dp)
    else:
        pl.semaphore_wait(barrier, n_dp)


    def image_rows(ref, b):
        return ref.at[at(b, seq)]

    def forward_self(b):
        load(image_rows(r.tokens, b), rows16, 0).wait()
        norm_forward(0, lambda span: rows16[span, :].astype(FULL), False)
        put = store(normed, image_rows(r.norm1, b), 0)
        put.start()
        wait_first(b, self_weights())

        @pl.when(b == 0)
        def _():
            start_all(kv_weights() + cross_weights() + down_weights())

        def project(j):
            proj[b, :, at(j, cols)] = dot_nn(normed[...], wide[:, at(j, cols)]).astype(LOW)

        loop(0, 3, project)
        made = [
            attend(proj[b, :, head(h)], proj[b, :, head(h, 1)], proj[b, :, head(h, 2)], None)
            for h in range(heads)
        ]
        for h, (mixed, weight) in enumerate(made):
            mix1[b, :, head(h)] = mixed
            prob1[b, h] = weight

        def out(c):
            part[b, :, at(c, cols)] = dot_nn(
                mix1[b], wide[at(c, cols), pl.ds(3 * cols, cols)]
            ).astype(LOW)

        loop(0, blocks, out)
        emit(b, piece)
        get = load(r.text.at[at(b, text_rows)], rows16.at[pl.ds(0, text_rows)], 0)
        get.start()

        def text_side():
            get.wait()
            wait_first(b, kv_weights())

            def key_value(j):
                kv2[b, :, at(j, cols)] = dot_nn(
                    rows16[pl.ds(0, text_rows), :], kv_w[:, at(j, cols)]
                ).astype(LOW)

            loop(0, 2, key_value)

        service(b, piece, piece, first=True, fill=(text_side, None))
        put.wait()
        pl.when(b + 1 < images)(lambda: load(image_rows(r.tokens, b + 1), rows16, 0).start())

    loop(0, images, forward_self)
    start_all(up_weights())

    def forward_cross(b):
        job = images + b
        get = load(image_rows(r.tokens, b), rows16, 0)
        get.start()
        settle(job - images, piece)
        get.wait()
        deep = mod(job - images, slots)
        norm_forward(
            1, lambda span: rows16[span, :].astype(FULL) + inbox[deep, span].astype(FULL), True
        )
        puts = [
            store(hid32, image_rows(r.after_self, b), 0),
            store(normed, image_rows(r.norm2, b), 1),
        ]
        start_all(puts)
        wait_first(b, cross_weights())
        q2[b] = dot_nn(normed[...], q_w[...]).astype(LOW)
        slot_at = lax.broadcasted_iota(jnp.int32, (1, text_rows), 1)
        valid = (slot_at < r.length[pl.ds(b, 1), :]) & (r.kept[pl.ds(b, 1), :] == 1)
        made = [
            attend(q2[b, :, head(h)], kv2[b, :, head(h)], kv2[b, :, head(h, 1)], valid)
            for h in range(heads)
        ]
        for h, (mixed, weight) in enumerate(made):
            mix2[b, :, head(h)] = mixed
            prob2[b, h] = weight

        def out(t):
            part[b, :, at(t, tile)] = dot_nn(mix2[b], o_w[:, at(t, tile)]).astype(LOW)

        loop(0, width // tile, out)
        emit(job, piece)
        service(job, piece, piece)
        wait_all(puts)

    loop(0, images, forward_cross)

    def feed_forward(b):
        job = 2 * images + b
        gets = [
            load(image_rows(r.after_self, b), hid32, 0),
            load(image_rows(r.cot, b), rows16, 1),
        ]
        start_all(gets)
        settle(job - images, piece)
        wait_all(gets)
        deep = mod(job - images, slots)
        norm_forward(2, lambda span: hid32[span, :] + inbox[deep, span].astype(FULL), True)
        puts = [
            store(hid32, image_rows(r.after_cross, b), 0),
            store(normed, image_rows(r.norm3, b), 1),
        ]
        start_all(puts)
        wait_first(b, up_weights() + down_weights())

        def middle(t):
            span = at(t, tile)
            pre = dot_nn(normed[...], wide[:, span]) + r.bias_up[:, span]
            curve = 0.5 * (1.0 + lax.erf(pre * 0.7071067811865476))
            active[:, span] = (pre * curve).astype(LOW)
            slope = curve + pre * jnp.exp(-0.5 * pre * pre) * 0.3989422804014327
            d_active = dot_nt(rows16[...], down[span, :]).astype(LOW).astype(FULL)
            d_low = (d_active * slope).astype(LOW)
            d_pre[:, span] = d_low
            sums[7:8, span] += jnp.sum(d_low.astype(FULL), axis=0, keepdims=True)

        loop(0, hidden // tile, middle)
        more = [
            store(active, image_rows(r.act_all, b), 2),
            store(d_pre, image_rows(r.pre_all, b), 3),
        ]
        start_all(more)

        def back(t):
            part[b, :, at(t, tile)] = dot_nt(d_pre[...], wide[at(t, tile), :]).astype(LOW)

        loop(0, width // tile, back)
        emit(job, piece)
        service(job, piece, piece)
        wait_all(puts + more)

    loop(0, images, feed_forward)
    start_all(self_weights())

    def feed_out(job, b):
        get = load(image_rows(r.act_all, b), active, 0)
        get.start()
        settle(job - images, piece)
        get.wait()
        slot = mod(job, images)

        def out(t):
            part[slot, :, at(t, tile)] = dot_nn(active[...], down[:, at(t, tile)]).astype(LOW)

        loop(0, width // tile, out)
        emit(job, piece)

    def out_load(b):
        return load(image_rows(r.after_cross, b), hid32, 0)

    def finish_out(job, b):
        out_load(b).wait()
        deep = mod(job, slots)

        def body(i):
            span = at(i, STEP)
            rows16[span, :] = (
                hid32[span, :] + inbox[deep, span].astype(FULL) + r.bias_down[...]
            ).astype(LOW)

        loop(0, seq // STEP, body)
        put = store(rows16, image_rows(r.layer_out, b), 2)
        put.start()
        put.wait()

    feed_out(3 * images, 0)
    service(3 * images, piece, piece, fill=(lambda: units(0, 0), None))

    def backward_cross(b):
        job = 3 * images + 1 + b
        gets = [
            load(image_rows(r.after_cross, b), hid32, 0),
            load(image_rows(r.cot, b), rows16, 1),
        ]
        start_all(gets)
        settle(job - images, piece)
        wait_all(gets)

        def base(span):
            top = rows16[span, :].astype(FULL)
            sums[6:7, :] += jnp.sum(top, axis=0, keepdims=True)
            return top

        norm_backward(2, lambda span: hid32[span, :], mod(2 * images + b, slots), base, True)
        puts = [
            store(grad32, image_rows(r.grad_rows, b), 0),
            store(normed, image_rows(r.low2, b), 1),
        ]
        start_all(puts)
        d_mix[...] = dot_nt(normed[...], o_w[...]).astype(LOW)
        pulled = [
            attend_back(
                d_mix[:, head(h)],
                q2[b, :, head(h)],
                kv2[b, :, head(h)],
                kv2[b, :, head(h, 1)],
                prob2[b, h],
            )
            for h in range(heads)
        ]
        for h, (d_query, d_key, d_value) in enumerate(pulled):
            q2[b, :, head(h)] = d_query
            kv2[b, :, head(h)] = d_key
            kv2[b, :, head(h, 1)] = d_value
        slot = mod(job, images)

        def out(t):
            part[slot, :, at(t, tile)] = dot_nt(q2[b], q_w[at(t, tile), :]).astype(LOW)

        loop(0, width // tile, out)
        emit(job, piece)
        service(job, piece, piece, fill=(lambda: units(1 + b, 0), None))
        wait_all(puts)

    loop(0, images, backward_cross)

    def second_out(b):
        job = 4 * images + b
        feed_out(job, b)

        @pl.when(b == 1)
        def _():
            out_load(0).start()
            finish_out(3 * images, 0)

        service(
            job,
            piece,
            piece,
            fill=(lambda: units(2 * b - 2, 1), lambda: units(2 * b - 1, 1)),
        )

    loop(1, images, second_out)

    def backward_self(b):
        job = 5 * images + b
        gets = [
            load(image_rows(r.after_self, b), hid32, 0),
            load(image_rows(r.grad_rows, b), grad32, 1),
        ]
        start_all(gets)
        settle(job - images, piece)
        wait_all(gets)
        norm_backward(
            1,
            lambda span: hid32[span, :],
            mod(3 * images + 1 + b, slots),
            lambda span: grad32[span, :],
            True,
        )
        puts = [
            store(grad32, image_rows(r.grad_rows, b), 0),
            store(normed, image_rows(r.low1, b), 1),
        ]
        start_all(puts)
        pl.when(b > 0)(lambda: out_load(b).start())
        wait_first(b, self_weights())
        total = None
        for c in range(blocks):
            term = dot_nt(
                normed[:, pl.ds(c * cols, cols)], wide[pl.ds(c * cols, cols), pl.ds(3 * cols, cols)]
            )
            total = term if total is None else total + term
        d_mix[...] = total.astype(LOW)
        pulled = [
            attend_back(
                d_mix[:, head(h)],
                proj[b, :, head(h)],
                proj[b, :, head(h, 1)],
                proj[b, :, head(h, 2)],
                prob1[b, h],
            )
            for h in range(heads)
        ]
        for h, (d_query, d_key, d_value) in enumerate(pulled):
            proj[b, :, head(h)] = d_query
            proj[b, :, head(h, 1)] = d_key
            proj[b, :, head(h, 2)] = d_value
        slot = mod(job, images)

        def out(t):
            part[slot, :, at(t, tile)] = dot_nt(
                proj[b], wide[at(t, tile), pl.ds(0, 3 * cols)]
            ).astype(LOW)

        loop(0, width // tile, out)
        emit(job, piece)
        service(
            job,
            piece,
            piece,
            fill=(lambda: units(b, 2), lambda: pl.when(b == images - 1)(lambda: units(3, 2))),
        )
        pl.when(b > 0)(lambda: finish_out(4 * images + b, b))
        wait_all(puts)

    loop(0, images, backward_self)

    for b in range(images):
        job = 6 * images + b
        gets = [
            load(image_rows(r.tokens, b), rows16, 0),
            load(image_rows(r.grad_rows, b), grad32, 1),
        ]
        start_all(gets)
        settle(job - images, piece)
        slot = mod(job, images)

        def out(t, slot=slot, b=b):
            part[slot, :text_rows, at(t, tile)] = dot_nt(kv2[b], kv_w[at(t, tile), :]).astype(LOW)

        loop(0, width // tile, out)
        emit(job, small)
        wait_all(gets)
        norm_backward(
            0,
            lambda span: rows16[span, :].astype(FULL),
            mod(5 * images + b, slots),
            lambda span: grad32[span, :],
            False,
        )
        put = store(grad32, image_rows(r.token_grad, b), 0)
        put.start()
        late = [
            (lambda: units(0, 3), lambda: units(1, 3)),
            (lambda: units(2, 3), lambda: units(3, 3)),
            (lambda: unit_finish(4 * chips - 1), lambda: unit_send(4 * chips - 1)),
        ]
        service(job, small, piece if b == 0 else small, fill=late[b])
        put.wait()

    def small_copy(hop):
        return pltpu.make_async_remote_copy(
            src_ref=sums,
            dst_ref=r.sums_in.at[member],
            send_sem=r.sum_send.at[hop],
            recv_sem=r.sum_recv.at[hop],
            device_id={"dp": lax.rem(member + hop, n_dp)},
            device_id_type=MESH,
        )

    for hop in range(1, n_dp):
        small_copy(hop).start()
    r.sums_in[member] = sums[...]

    last = 7 * images - 1
    fold(last, 2, small)
    fold(last, 3, small)
    for p in range(PIECES):
        spread(last, p, small)
    for b in range(images):
        job = 6 * images + b
        settle(job, small)
        put = store(
            inbox.at[mod(job, slots), pl.ds(0, text_rows)],
            r.text_sum.at[at(b, text_rows)],
            b,
        )
        put.start()
        put.wait()

    for hop in range(1, n_dp):
        small_copy(hop).wait()
    whole = r.sums_in[0]
    for d in range(1, n_dp):
        whole = whole + r.sums_in[d]
    r.sums_out[...] = whole

    for q in range(4):
        for far in range(1, chips):
            chip_copy(q * chips + far - 1, q, far).wait()


class Ends(NamedTuple):
    layer_out: Any
    token_grad: Any
    text_grad: Any
    w_self: Any
    wo_self: Any
    wq: Any
    wkv: Any
    wo_cross: Any
    w_up: Any
    bias_up: Any
    w_down: Any
    bias_down: Any
    gain: Any
    shift: Any


class Held(NamedTuple):
    shares: Any
    text_low: Any
    text: Any
    token_grad: Any
    layer_out: Any
    w_self: Any
    wo_self: Any
    wq: Any
    wkv: Any
    wo_cross: Any
    w_up: Any
    w_down: Any
    load_sem: Any
    put_sem: Any


def closing_kernel(chips, cols, shares, token_grad, layer_out, text_sum, sums, *refs):
    ends = Ends(*refs[: len(Ends._fields)])
    held = Held(*refs[len(Ends._fields) :])
    parts = shares.shape[3] // cols
    text_load = pltpu.make_async_copy(text_sum, held.text_low, held.load_sem.at[4 * chips])
    loads = [
        [
            pltpu.make_async_copy(
                shares.at[q, c], held.shares.at[q, c], held.load_sem.at[q * chips + c]
            )
            for c in range(chips)
        ]
        for q in range(4)
    ]
    puts = []

    def put(src, dst):
        copy = pltpu.make_async_copy(src, dst, held.put_sem.at[len(puts)])
        copy.start()
        puts.append(copy)

    for q in range(4):
        for copy in loads[q]:
            copy.start()
    more = [
        pltpu.make_async_copy(token_grad, held.token_grad, held.load_sem.at[4 * chips + 1]),
        pltpu.make_async_copy(layer_out, held.layer_out, held.load_sem.at[4 * chips + 2]),
    ]
    for copy in more:
        copy.start()
    text_load.start()
    ends.bias_up[...] = sums[7:8, : ends.bias_up.shape[1]]
    ends.bias_down[...] = sums[6:7, :]
    ends.gain[...] = sums[0:3, :]
    ends.shift[...] = sums[3:6, :]

    def total(q, j):
        span = pl.ds(j * cols, cols)
        whole = held.shares[q, 0, :, span].astype(FULL)
        for c in range(1, chips):
            whole = whole + held.shares[q, c, :, span].astype(FULL)
        return whole

    for q in range(4):
        for copy in loads[q]:
            copy.wait()
        for j in range(parts):
            whole = total(q, j)
            if q == 0:
                held.w_down[pl.ds(j * cols, cols), :] = whole.T
            elif q == 1:
                held.w_up[:, pl.ds(j * cols, cols)] = whole
            elif j == 0:
                (held.wo_cross if q == 2 else held.wo_self)[...] = whole.T
            elif q == 3:
                held.w_self[j - 1] = whole
            elif j == 1:
                held.wq[...] = whole
            else:
                held.wkv[j - 2] = whole
        if q == 0:
            put(held.w_down, ends.w_down)
        elif q == 1:
            put(held.w_up, ends.w_up)
        elif q == 2:
            put(held.wo_cross, ends.wo_cross)
            put(held.wq, ends.wq)
            put(held.wkv, ends.wkv)
        else:
            put(held.wo_self, ends.wo_self)
            put(held.w_self, ends.w_self)
    more[0].wait()
    put(held.token_grad, ends.token_grad)
    more[1].wait()
    put(held.layer_out, ends.layer_out)
    text_load.wait()
    held.text[...] = held.text_low[...].astype(FULL)
    put(held.text, ends.text_grad)
    for copy in puts:
        copy.wait()


def local(
    n_mp,
    n_dp,
    tokens,
    text,
    text_len,
    text_mask,
    cotangent,
    w_self,
    wo_self,
    wq_cross,
    wkv_cross,
    wo_cross,
    w_up,
    bias_up,
    w_down,
    bias_down,
    ln_gain,
    ln_bias,
):
    images, seq, width = tokens.shape
    text_rows = text.shape[1]
    cols = w_self.shape[2]
    hidden = w_up.shape[1]
    heads = cols // HEAD_DIM
    rows = images * seq
    chips = n_dp // 2
    block = width // n_dp
    tile = min(512, hidden, width)

    def out(*shape, kind=LOW):
        return jax.ShapeDtypeStruct(shape, kind)

    outs = Outputs(
        layer_out=out(rows, width),
        token_grad=out(rows, width, kind=FULL),
        text_sum=out(images * text_rows, width),
        shares=out(4, chips, block, hidden),
        sums_out=out(8, width, kind=FULL),
        norm1=out(rows, width),
        norm2=out(rows, width),
        norm3=out(rows, width),
        low1=out(rows, width),
        low2=out(rows, width),
        act_all=out(rows, hidden),
        pre_all=out(rows, hidden),
        after_self=out(rows, width, kind=FULL),
        after_cross=out(rows, width, kind=FULL),
        grad_rows=out(rows, width, kind=FULL),
        staged=out(4 * chips, block, hidden),
    )
    slots = 2 * images

    def buf(*shape, kind=LOW):
        return pltpu.VMEM(shape, kind)

    dma = pltpu.SemaphoreType.DMA
    scratch = Scratch(
        wide=buf(width, hidden),
        down=buf(hidden, width),
        kv_w=buf(width, 2 * cols),
        q_w=buf(width, cols),
        o_w=buf(cols, width),
        inbox=buf(slots, seq, width),
        outbox=buf(images, seq, width),
        part=buf(images, seq, width),
        proj=buf(images, seq, 3 * cols),
        mix1=buf(images, seq, cols),
        prob1=buf(images, heads, seq, seq),
        q2=buf(images, seq, cols),
        kv2=buf(images, text_rows, 2 * cols),
        mix2=buf(images, seq, cols),
        prob2=buf(images, heads, seq, text_rows),
        hid32=buf(seq, width, kind=FULL),
        grad32=buf(seq, width, kind=FULL),
        normed=buf(seq, width),
        rows16=buf(seq, width),
        d_pre=buf(seq, hidden),
        active=buf(seq, hidden),
        d_mix=buf(seq, cols),
        tile=buf(2 * block, hidden),
        tile_sum=buf(block, hidden),
        tile_in=buf(2, block, hidden),
        unit_cols=buf(3, rows, max(tile, 2 * block)),
        x_text=buf(images * text_rows, 2 * block),
        sums=buf(8, width, kind=FULL),
        sums_in=buf(n_dp, 8, width, kind=FULL),
        send_sem=dma((images, PIECES)),
        out_sem=dma((images, PIECES)),
        in_sem=dma((slots, PIECES)),
        pass_sem=dma((slots, PIECES)),
        weight_sem=dma((3 + width // cols + 5,)),
        load_sem=dma((2,)),
        store_sem=dma((4,)),
        unit_sem=dma((6,)),
        core_send=dma((4 * chips,)),
        core_recv=dma((4 * chips,)),
        chip_send=dma((4 * chips,)),
        chip_recv=dma((4, chips)),
        sum_send=dma((n_dp,)),
        sum_recv=dma((n_dp,)),
    )
    vmem = pl.BlockSpec(memory_space=pltpu.VMEM)
    anywhere = pl.BlockSpec(memory_space=pl.ANY)
    sizes = (n_mp, n_dp, images, seq, width, text_rows, cols, hidden)
    results = pl.pallas_call(
        functools.partial(layer_kernel, sizes),
        out_shape=tuple(outs),
        in_specs=list(
            Inputs(*[anywhere] * len(Inputs._fields))._replace(
                length=vmem, kept=vmem, bias_up=vmem, bias_down=vmem, gain=vmem, shift=vmem
            )
        ),
        out_specs=tuple(Outputs(*[anywhere] * len(outs))._replace(sums_out=vmem)),
        scratch_shapes=list(scratch),
        compiler_params=pltpu.CompilerParams(
            collective_id=0, has_side_effects=True, vmem_limit_bytes=VMEM_LIMIT
        ),
        name="layer",
    )(
        tokens.reshape(rows, width),
        text.reshape(images * text_rows, width),
        text_len.reshape(images, 1),
        text_mask,
        cotangent.reshape(rows, width),
        w_self,
        wo_self,
        wq_cross,
        wkv_cross,
        wo_cross,
        w_up,
        bias_up.reshape(1, hidden),
        w_down,
        bias_down.reshape(1, width),
        ln_gain,
        ln_bias,
    )
    got = Outputs(*results)
    shapes = Ends(
        layer_out=out(rows, width),
        token_grad=out(rows, width, kind=FULL),
        text_grad=out(images * text_rows, width, kind=FULL),
        w_self=out(3, block, cols, kind=FULL),
        wo_self=out(cols, block, kind=FULL),
        wq=out(block, cols, kind=FULL),
        wkv=out(2, block, cols, kind=FULL),
        wo_cross=out(cols, block, kind=FULL),
        w_up=out(block, hidden, kind=FULL),
        bias_up=out(1, hidden, kind=FULL),
        w_down=out(hidden, block, kind=FULL),
        bias_down=out(1, width, kind=FULL),
        gain=out(3, width, kind=FULL),
        shift=out(3, width, kind=FULL),
    )
    staging = Held(
        shares=buf(4, chips, block, hidden),
        text_low=buf(images * text_rows, width),
        text=buf(images * text_rows, width, kind=FULL),
        token_grad=buf(rows, width, kind=FULL),
        layer_out=buf(rows, width),
        w_self=buf(3, block, cols, kind=FULL),
        wo_self=buf(cols, block, kind=FULL),
        wq=buf(block, cols, kind=FULL),
        wkv=buf(2, block, cols, kind=FULL),
        wo_cross=buf(cols, block, kind=FULL),
        w_up=buf(block, hidden, kind=FULL),
        w_down=buf(hidden, block, kind=FULL),
        load_sem=dma((4 * chips + 3,)),
        put_sem=dma((10,)),
    )
    ends = Ends(
        *pl.pallas_call(
            functools.partial(closing_kernel, chips, cols),
            out_shape=tuple(shapes),
            in_specs=[anywhere] * 4 + [vmem],
            out_specs=tuple(
                Ends(*[anywhere] * len(shapes))._replace(
                    bias_up=vmem, bias_down=vmem, gain=vmem, shift=vmem
                )
            ),
            scratch_shapes=list(staging),
            compiler_params=pltpu.CompilerParams(vmem_limit_bytes=VMEM_LIMIT),
            name="closing",
        )(got.shares, got.token_grad, got.layer_out, got.text_sum, got.sums_out)
    )
    return (
        ends.layer_out.reshape(images, seq, width),
        ends.token_grad.reshape(images, seq, width),
        ends.text_grad.reshape(images, text_rows, width),
        ends.w_self,
        ends.wo_self,
        ends.wq,
        ends.wkv,
        ends.wo_cross,
        ends.w_up,
        ends.bias_up.reshape(hidden),
        ends.w_down,
        ends.bias_down.reshape(width),
        ends.gain,
        ends.shift,
    )


def solution(mesh):
    placed = (
        P("dp", None, None),
        P("dp", None, None),
        P("dp"),
        P("dp", None),
        P("dp", None, None),
        P(None, None, "mp"),
        P("mp", None),
        P(None, "mp"),
        P(None, None, "mp"),
        P("mp", None),
        P(None, "mp"),
        P("mp"),
        P("mp", None),
        P(),
        P(),
        P(),
    )
    return jax.shard_map(
        functools.partial(local, mesh.shape["mp"], mesh.shape["dp"]),
        mesh=mesh,
        in_specs=placed,
        out_specs=(
            P("dp", None, None),
            P("dp", None, None),
            P("dp", None, None),
            P(None, "dp", "mp"),
            P("mp", "dp"),
            P("dp", "mp"),
            P(None, "dp", "mp"),
            P("mp", "dp"),
            P("dp", "mp"),
            P("mp"),
            P("mp", "dp"),
            P(),
            P(),
            P(),
        ),
        check_vma=False,
    )
```

```python
import functools
from typing import Any, NamedTuple

import jax
import jax.numpy as jnp
from jax import lax
from jax.experimental import pallas as pl
from jax.experimental.pallas import tpu as pltpu
from jax.sharding import PartitionSpec as P

HEAD_DIM = 128
MASKED = -1e30
NORM_EPS = 1e-05
PIECES = 4
STEP = 32
LOW = jnp.bfloat16
FULL = jnp.float32
MESH = pl.DeviceIdType.MESH
VMEM_LIMIT = 64 * 1024 * 1024 - 512 * 1024

class Inputs(NamedTuple):
    tokens: Any
    text: Any
    length: Any
    kept: Any
    cot: Any
    w_self: Any
    wo_self: Any
    wq: Any
    wkv: Any
    wo_cross: Any
    w_up: Any
    bias_up: Any
    w_down: Any
    bias_down: Any
    gain: Any
    shift: Any


class Outputs(NamedTuple):
    layer_out: Any
    token_grad: Any
    text_sum: Any
    shares: Any
    sums_out: Any
    norm1: Any
    norm2: Any
    norm3: Any
    low1: Any
    low2: Any
    act_all: Any
    pre_all: Any
    after_self: Any
    after_cross: Any
    grad_rows: Any
    staged: Any


class Scratch(NamedTuple):
    wide: Any
    down: Any
    kv_w: Any
    q_w: Any
    o_w: Any
    inbox: Any
    outbox: Any
    part: Any
    proj: Any
    mix1: Any
    prob1: Any
    q2: Any
    kv2: Any
    mix2: Any
    prob2: Any
    hid32: Any
    grad32: Any
    normed: Any
    rows16: Any
    d_pre: Any
    active: Any
    d_mix: Any
    tile: Any
    tile_sum: Any
    tile_in: Any
    unit_cols: Any
    x_text: Any
    sums: Any
    sums_in: Any
    send_sem: Any
    out_sem: Any
    in_sem: Any
    pass_sem: Any
    weight_sem: Any
    load_sem: Any
    store_sem: Any
    unit_sem: Any
    core_send: Any
    core_recv: Any
    chip_send: Any
    chip_recv: Any
    sum_send: Any
    sum_recv: Any


class Refs(NamedTuple):
    tokens: Any
    text: Any
    length: Any
    kept: Any
    cot: Any
    w_self: Any
    wo_self: Any
    wq: Any
    wkv: Any
    wo_cross: Any
    w_up: Any
    bias_up: Any
    w_down: Any
    bias_down: Any
    gain: Any
    shift: Any
    layer_out: Any
    token_grad: Any
    text_sum: Any
    shares: Any
    sums_out: Any
    norm1: Any
    norm2: Any
    norm3: Any
    low1: Any
    low2: Any
    act_all: Any
    pre_all: Any
    after_self: Any
    after_cross: Any
    grad_rows: Any
    staged: Any
    wide: Any
    down: Any
    kv_w: Any
    q_w: Any
    o_w: Any
    inbox: Any
    outbox: Any
    part: Any
    proj: Any
    mix1: Any
    prob1: Any
    q2: Any
    kv2: Any
    mix2: Any
    prob2: Any
    hid32: Any
    grad32: Any
    normed: Any
    rows16: Any
    d_pre: Any
    active: Any
    d_mix: Any
    tile: Any
    tile_sum: Any
    tile_in: Any
    unit_cols: Any
    x_text: Any
    sums: Any
    sums_in: Any
    send_sem: Any
    out_sem: Any
    in_sem: Any
    pass_sem: Any
    weight_sem: Any
    load_sem: Any
    store_sem: Any
    unit_sem: Any
    core_send: Any
    core_recv: Any
    chip_send: Any
    chip_recv: Any
    sum_send: Any
    sum_recv: Any


def dot_nn(left, right):
    return jnp.dot(left, right, preferred_element_type=FULL)


def dot_nt(left, right):
    return lax.dot_general(left, right, (((1,), (1,)), ((), ())), preferred_element_type=FULL)


def dot_tn(left, right):
    return lax.dot_general(left, right, (((0,), (0,)), ((), ())), preferred_element_type=FULL)


def mod(value, size):
    return value % size if isinstance(value, int) else lax.rem(value, size)


def at(index, size):
    return pl.ds(pl.multiple_of(index * size, size), size)


def loop(start, stop, body):
    def step(index, carry):
        body(index)
        return carry

    lax.fori_loop(start, stop, step, 0)


def layer_kernel(sizes, *refs):
    r = Refs(*refs)
    n_mp, n_dp, images, seq, width, text_rows, cols, hidden = sizes
    heads = cols // HEAD_DIM
    scale = HEAD_DIM**-0.5
    half = n_mp // 2
    slots = 2 * images
    piece = seq // PIECES
    small = text_rows // PIECES
    chips = n_dp // 2
    block = width // n_dp
    tile = min(512, hidden, width)
    wide, down, kv_w, q_w, o_w = r.wide, r.down, r.kv_w, r.q_w, r.o_w
    inbox, outbox, part = r.inbox, r.outbox, r.part
    hid32, grad32, normed, rows16 = r.hid32, r.grad32, r.normed, r.rows16
    proj, mix1, prob1, q2, kv2 = r.proj, r.mix1, r.prob1, r.q2, r.kv2
    mix2, prob2, d_pre, active, d_mix = r.mix2, r.prob2, r.d_pre, r.active, r.d_mix
    sums = r.sums
    place = lax.axis_index("mp")
    member = lax.axis_index("dp")
    core = lax.rem(member, 2)
    chip = lax.div(member, 2)
    low_half = place < half
    at_end = (place == 0) | (place == n_mp - 1)
    not_end = jnp.logical_not(at_end)
    at_mid = (place == half - 1) | (place == half)
    inner = jnp.where(low_half, place + 1, place - 1)
    outer = jnp.where(at_end, place, jnp.where(low_half, place - 1, place + 1))

    def load(src, dst, index):
        return pltpu.make_async_copy(src, dst, r.load_sem.at[index])

    def store(src, dst, index):
        return pltpu.make_async_copy(src, dst, r.store_sem.at[index])

    blocks = width // cols

    def self_weights():
        made = [
            pltpu.make_async_copy(
                r.w_self.at[j], wide.at[:, pl.ds(j * cols, cols)], r.weight_sem.at[j]
            )
            for j in range(3)
        ]
        for c in range(blocks):
            made.append(
                pltpu.make_async_copy(
                    r.wo_self.at[:, pl.ds(c * cols, cols)],
                    wide.at[pl.ds(c * cols, cols), pl.ds(3 * cols, cols)],
                    r.weight_sem.at[3 + c],
                )
            )
        return made

    other = 3 + blocks

    def up_weights():
        return [pltpu.make_async_copy(r.w_up, wide, r.weight_sem.at[0])]

    def down_weights():
        return [pltpu.make_async_copy(r.w_down, down, r.weight_sem.at[other])]

    def kv_weights():
        return [
            pltpu.make_async_copy(
                r.wkv.at[j], kv_w.at[:, pl.ds(j * cols, cols)], r.weight_sem.at[other + 1 + j]
            )
            for j in range(2)
        ]

    def cross_weights():
        return [
            pltpu.make_async_copy(r.wq, q_w, r.weight_sem.at[other + 3]),
            pltpu.make_async_copy(r.wo_cross, o_w, r.weight_sem.at[other + 4]),
        ]

    def start_all(copies):
        for copy in copies:
            copy.start()

    def wait_all(copies):
        for copy in copies:
            copy.wait()

    def wait_first(index, copies):
        @pl.when(index == 0)
        def _():
            wait_all(copies)

    def sum_copy(job, p, rows, swap):
        span = pl.ds(p * rows, rows)
        slot, deep = mod(job, images), mod(job, slots)
        return pltpu.make_async_remote_copy(
            src_ref=part.at[slot, span],
            dst_ref=inbox.at[deep, span] if swap else outbox.at[slot, span],
            send_sem=r.send_sem.at[slot, p],
            recv_sem=r.in_sem.at[deep, p] if swap else r.out_sem.at[slot, p],
            device_id={"mp": inner},
            device_id_type=MESH,
        )

    def pass_copy(job, p, rows):
        span = pl.ds(p * rows, rows)
        deep = mod(job, slots)
        return pltpu.make_async_remote_copy(
            src_ref=inbox.at[deep, span],
            dst_ref=inbox.at[deep, span],
            send_sem=r.pass_sem.at[deep, p],
            recv_sem=r.in_sem.at[deep, p],
            device_id={"mp": outer},
            device_id_type=MESH,
        )

    def emit(job, rows):
        @pl.when(at_end)
        def _():
            for p in range(PIECES):
                sum_copy(job, p, rows, half == 1).start()

    def fold(job, p, rows):
        if half == 1:
            return
        span = pl.ds(p * rows, rows)
        slot = mod(job, images)

        @pl.when(not_end)
        def _():
            sum_copy(job, p, rows, False).wait_recv()
            part[slot, span] = part[slot, span] + outbox[slot, span]

        @pl.when(at_mid)
        def _():
            sum_copy(job, p, rows, True).start()

        if half > 2:

            @pl.when(jnp.logical_not(at_mid | at_end))
            def _():
                sum_copy(job, p, rows, False).start()

    def spread(job, p, rows):
        span = pl.ds(p * rows, rows)
        slot, deep = mod(job, images), mod(job, slots)

        @pl.when(at_mid)
        def _():
            pass_copy(job, p, rows).wait_recv()
            inbox[deep, span] = part[slot, span] + inbox[deep, span]

        if half > 2:

            @pl.when(jnp.logical_not(at_mid | at_end))
            def _():
                pass_copy(job, p, rows).wait_recv()

        if half > 1:

            @pl.when(not_end)
            def _():
                pass_copy(job, p, rows).start()

    def settle(job, rows):
        for p in range(PIECES):
            sum_copy(job, p, rows, False).wait_send()
        if half > 1:

            @pl.when(not_end)
            def _():
                for p in range(PIECES):
                    pass_copy(job, p, rows).wait_send()

            @pl.when(at_end)
            def _():
                for p in range(PIECES):
                    pass_copy(job, p, rows).wait_recv()

    def service(job, rows, before, first=False, fill=(None, None)):
        def run(body):
            if first:
                pl.when(job > 0)(body)
            else:
                body()

        @run
        def _():
            fold(job - 1, 2, before)
            fold(job - 1, 3, before)
            spread(job - 1, 0, before)
            spread(job - 1, 1, before)

        if fill[0]:
            fill[0]()
        fold(job, 0, rows)

        @run
        def _():
            spread(job - 1, 2, before)

        if fill[1]:
            fill[1]()
        fold(job, 1, rows)

        @run
        def _():
            spread(job - 1, 3, before)

    def norm_stats(x):
        mean = jnp.mean(x, axis=-1, keepdims=True)
        centred = x - mean
        var = jnp.mean(centred * centred, axis=-1, keepdims=True)
        inv = lax.rsqrt(var + NORM_EPS)
        return centred * inv, inv

    def norm_forward(which, read, keep):
        def body(i):
            span = at(i, STEP)
            x = read(span)
            unit, _ = norm_stats(x)
            if keep:
                hid32[span, :] = x
            normed[span, :] = (
                unit * r.gain[which : which + 1, :] + r.shift[which : which + 1, :]
            ).astype(LOW)

        loop(0, seq // STEP, body)

    def norm_backward(which, read, deep, base, low):
        def body(i):
            span = at(i, STEP)
            unit, inv = norm_stats(read(span))
            grad = inbox[deep, span].astype(FULL)
            sums[which : which + 1, :] += jnp.sum(grad * unit, axis=0, keepdims=True)
            sums[3 + which : 4 + which, :] += jnp.sum(grad, axis=0, keepdims=True)
            scaled = grad * r.gain[which : which + 1, :]
            back = inv * (
                scaled
                - jnp.mean(scaled, axis=-1, keepdims=True)
                - unit * jnp.mean(scaled * unit, axis=-1, keepdims=True)
            )
            whole = base(span) + back
            grad32[span, :] = whole
            if low:
                normed[span, :] = whole.astype(LOW)

        loop(0, seq // STEP, body)

    def attend(queries, keys, values, valid):
        scores = dot_nt(queries, keys) * scale
        if valid is not None:
            scores = jnp.where(valid, scores, MASKED)
        powers = jnp.exp(scores - jnp.max(scores, axis=-1, keepdims=True))
        weight = (powers / jnp.sum(powers, axis=-1, keepdims=True)).astype(LOW)
        return dot_nn(weight, values).astype(LOW), weight

    def attend_back(d_out, queries, keys, values, weight):
        prob = weight.astype(FULL)
        d_weight = dot_nt(d_out, values)
        d_value = dot_tn(weight, d_out)
        d_score = (
            prob * (d_weight - jnp.sum(d_weight * prob, axis=-1, keepdims=True))
        ).astype(LOW)
        d_query = dot_nn(d_score, keys) * scale
        d_key = dot_tn(d_score, queries) * scale
        return d_query.astype(LOW), d_key.astype(LOW), d_value.astype(LOW)

    def head(h, group=0):
        return pl.ds(group * cols + h * HEAD_DIM, HEAD_DIM)

    def chip_at(far):
        down_y = lax.rem(lax.div(chip, 2) + far // 2, chips // 2)
        return 2 * down_y + lax.rem(lax.rem(chip, 2) + far % 2, 2)

    def core_copy(turn):
        return pltpu.make_async_remote_copy(
            src_ref=r.tile.at[at(1 - core, block)],
            dst_ref=r.tile_in.at[mod(turn, 2)],
            send_sem=r.core_send.at[turn],
            recv_sem=r.core_recv.at[turn],
            device_id={"dp": member + 1 - 2 * core},
            device_id_type=MESH,
        )

    def chip_copy(turn, q, far):
        return pltpu.make_async_remote_copy(
            src_ref=r.staged.at[turn],
            dst_ref=r.shares.at[q, far],
            send_sem=r.chip_send.at[turn],
            recv_sem=r.chip_recv.at[q, far],
            device_id={"dp": 2 * chip_at(far) + core},
            device_id_type=MESH,
        )

    def unit_finish(turn):
        q, i = lax.div(turn, chips), lax.rem(turn, chips)
        slot = lax.rem(turn, 2)
        core_copy(turn).wait()

        def body(k):
            span = at(k, STEP)
            own = pl.ds(pl.multiple_of(core * block + k * STEP, STEP), STEP)
            r.tile_sum[span, :] = r.tile[own, :] + r.tile_in[slot, span]

        loop(0, block // STEP, body)

        @pl.when(i == chips - 1)
        def _():
            pltpu.make_async_copy(r.tile_sum, r.shares.at[q, 0], r.unit_sem.at[5]).start()

        @pl.when(i < chips - 1)
        def _():
            pltpu.make_async_copy(r.tile_sum, r.staged.at[turn], r.unit_sem.at[5]).start()

    def unit_send(turn):
        q, i = lax.div(turn, chips), lax.rem(turn, chips)
        pltpu.make_async_copy(r.tile_sum, r.staged.at[turn], r.unit_sem.at[5]).wait()

        @pl.when(i < chips - 1)
        def _():
            chip_copy(turn, q, i + 1).start()

    rows_all = images * seq
    text_all = images * text_rows

    def unit(q, i):
        turn = q * chips + i
        target = chip_at(mod(i + 1, chips))

        def x_load(which, src):
            return pltpu.make_async_copy(
                src.at[:, at(target, 2 * block)],
                r.x_text if which == 2 else r.unit_cols.at[which, :, pl.ds(0, 2 * block)],
                r.unit_sem.at[which],
            )

        def y_load(src, t):
            return pltpu.make_async_copy(
                src.at[:, pl.ds(t * tile, tile)],
                r.unit_cols.at[1 + t % 2, :, pl.ds(0, tile)],
                r.unit_sem.at[3 + t % 2],
            )

        def held(ref, rows, start):
            return ref[:, :, pl.ds(start, cols)].reshape(rows, cols)

        if q < 2:
            xs = [x_load(0, r.norm3 if q else r.cot)]
            ys = [y_load(r.pre_all if q else r.act_all, t) for t in range(hidden // tile)]
            start_all(ys[:2])
        elif q == 2:
            xs = [x_load(0, r.low2), x_load(1, r.norm2), x_load(2, r.text)]
        else:
            xs = [x_load(0, r.low1), x_load(1, r.norm1)]
        start_all(xs)

        @pl.when(turn > 0)
        def _():
            unit_finish(turn - 1)

        wait_all(xs)

        def turned(which):
            return r.unit_cols[which, :, : 2 * block].T

        def put(offset, left, right):
            r.tile[:, pl.ds(offset, right.shape[1])] = dot_nn(left, right).astype(LOW)

        if q < 2:
            left = turned(0)
            for t, copy in enumerate(ys):
                copy.wait()
                put(t * tile, left, r.unit_cols[1 + t % 2, :, :tile])
                if t + 2 < len(ys):
                    ys[t + 2].start()
        elif q == 2:
            put(0, turned(0), held(mix2, rows_all, 0))
            put(cols, turned(1), held(q2, rows_all, 0))
            left = r.x_text[...].T
            for j in range(2):
                put((2 + j) * cols, left, held(kv2, text_all, j * cols))
        else:
            put(0, turned(0), held(mix1, rows_all, 0))
            left = turned(1)
            for j in range(3):
                put((1 + j) * cols, left, held(proj, rows_all, j * cols))
        core_copy(turn).start()

        @pl.when(turn > 0)
        def _():
            unit_send(turn - 1)

    quarter = chips // 4

    def units(b, q):
        loop(b * quarter, (b + 1) * quarter, functools.partial(unit, q))

    first_rows = load(r.tokens.at[pl.ds(0, seq)], rows16, 0)
    first_rows.start()
    start_all(self_weights())
    sums[...] = jnp.zeros_like(sums)

    barrier = pltpu.get_barrier_semaphore()
    for hop in range(1, n_dp):
        pl.semaphore_signal(
            barrier, inc=1, device_id={"dp": lax.rem(member + hop, n_dp)}, device_id_type=MESH
        )
    pl.semaphore_signal(barrier, inc=1, device_id={"mp": inner}, device_id_type=MESH)
    if half > 1:

        @pl.when(not_end)
        def _():
            pl.semaphore_signal(barrier, inc=1, device_id={"mp": outer}, device_id_type=MESH)
            pl.semaphore_wait(barrier, n_dp + 1)

        @pl.when(at_end)
        def _():
            pl.semaphore_wait(barrier, n_dp)
    else:
        pl.semaphore_wait(barrier, n_dp)


    def image_rows(ref, b):
        return ref.at[at(b, seq)]

    def forward_self(b):
        load(image_rows(r.tokens, b), rows16, 0).wait()
        norm_forward(0, lambda span: rows16[span, :].astype(FULL), False)
        put = store(normed, image_rows(r.norm1, b), 0)
        put.start()
        wait_first(b, self_weights())

        @pl.when(b == 0)
        def _():
            start_all(kv_weights() + cross_weights() + down_weights())

        def project(j):
            proj[b, :, at(j, cols)] = dot_nn(normed[...], wide[:, at(j, cols)]).astype(LOW)

        loop(0, 3, project)
        made = [
            attend(proj[b, :, head(h)], proj[b, :, head(h, 1)], proj[b, :, head(h, 2)], None)
            for h in range(heads)
        ]
        for h, (mixed, weight) in enumerate(made):
            mix1[b, :, head(h)] = mixed
            prob1[b, h] = weight

        def out(c):
            part[b, :, at(c, cols)] = dot_nn(
                mix1[b], wide[at(c, cols), pl.ds(3 * cols, cols)]
            ).astype(LOW)

        loop(0, blocks, out)
        emit(b, piece)
        get = load(r.text.at[at(b, text_rows)], rows16.at[pl.ds(0, text_rows)], 0)
        get.start()

        def text_side():
            get.wait()
            wait_first(b, kv_weights())

            def key_value(j):
                kv2[b, :, at(j, cols)] = dot_nn(
                    rows16[pl.ds(0, text_rows), :], kv_w[:, at(j, cols)]
                ).astype(LOW)

            loop(0, 2, key_value)

        service(b, piece, piece, first=True, fill=(text_side, None))
        put.wait()
        pl.when(b + 1 < images)(lambda: load(image_rows(r.tokens, b + 1), rows16, 0).start())

    loop(0, images, forward_self)
    start_all(up_weights())

    def forward_cross(b):
        job = images + b
        get = load(image_rows(r.tokens, b), rows16, 0)
        get.start()
        settle(job - images, piece)
        get.wait()
        deep = mod(job - images, slots)
        norm_forward(
            1, lambda span: rows16[span, :].astype(FULL) + inbox[deep, span].astype(FULL), True
        )
        puts = [
            store(hid32, image_rows(r.after_self, b), 0),
            store(normed, image_rows(r.norm2, b), 1),
        ]
        start_all(puts)
        wait_first(b, cross_weights())
        q2[b] = dot_nn(normed[...], q_w[...]).astype(LOW)
        slot_at = lax.broadcasted_iota(jnp.int32, (1, text_rows), 1)
        image_at = lax.broadcasted_iota(jnp.int32, (1, images), 1)
        length = jnp.sum(
            jnp.where(image_at == b, r.length[...], 0), axis=1, keepdims=True, dtype=jnp.int32
        )
        valid = (slot_at < length) & (r.kept[pl.ds(b, 1), :] == 1)
        made = [
            attend(q2[b, :, head(h)], kv2[b, :, head(h)], kv2[b, :, head(h, 1)], valid)
            for h in range(heads)
        ]
        for h, (mixed, weight) in enumerate(made):
            mix2[b, :, head(h)] = mixed
            prob2[b, h] = weight

        def out(t):
            part[b, :, at(t, tile)] = dot_nn(mix2[b], o_w[:, at(t, tile)]).astype(LOW)

        loop(0, width // tile, out)
        emit(job, piece)
        service(job, piece, piece)
        wait_all(puts)

    loop(0, images, forward_cross)

    def feed_forward(b):
        job = 2 * images + b
        gets = [
            load(image_rows(r.after_self, b), hid32, 0),
            load(image_rows(r.cot, b), rows16, 1),
        ]
        start_all(gets)
        settle(job - images, piece)
        wait_all(gets)
        deep = mod(job - images, slots)
        norm_forward(2, lambda span: hid32[span, :] + inbox[deep, span].astype(FULL), True)
        puts = [
            store(hid32, image_rows(r.after_cross, b), 0),
            store(normed, image_rows(r.norm3, b), 1),
        ]
        start_all(puts)
        wait_first(b, up_weights() + down_weights())

        def middle(t):
            span = at(t, tile)
            pre = dot_nn(normed[...], wide[:, span]) + r.bias_up[:, span]
            curve = 0.5 * (1.0 + lax.erf(pre * 0.7071067811865476))
            active[:, span] = (pre * curve).astype(LOW)
            slope = curve + pre * jnp.exp(-0.5 * pre * pre) * 0.3989422804014327
            d_active = dot_nt(rows16[...], down[span, :]).astype(LOW).astype(FULL)
            d_low = (d_active * slope).astype(LOW)
            d_pre[:, span] = d_low
            sums[7:8, span] += jnp.sum(d_low.astype(FULL), axis=0, keepdims=True)

        loop(0, hidden // tile, middle)
        more = [
            store(active, image_rows(r.act_all, b), 2),
            store(d_pre, image_rows(r.pre_all, b), 3),
        ]
        start_all(more)

        def back(t):
            part[b, :, at(t, tile)] = dot_nt(d_pre[...], wide[at(t, tile), :]).astype(LOW)

        loop(0, width // tile, back)
        emit(job, piece)
        service(job, piece, piece)
        wait_all(puts + more)

    loop(0, images, feed_forward)
    start_all(self_weights())

    def feed_out(job, b):
        get = load(image_rows(r.act_all, b), active, 0)
        get.start()
        settle(job - images, piece)
        get.wait()
        slot = mod(job, images)

        def out(t):
            part[slot, :, at(t, tile)] = dot_nn(active[...], down[:, at(t, tile)]).astype(LOW)

        loop(0, width // tile, out)
        emit(job, piece)

    def out_load(b):
        return load(image_rows(r.after_cross, b), hid32, 0)

    def finish_out(job, b):
        out_load(b).wait()
        deep = mod(job, slots)

        def body(i):
            span = at(i, STEP)
            rows16[span, :] = (
                hid32[span, :] + inbox[deep, span].astype(FULL) + r.bias_down[...]
            ).astype(LOW)

        loop(0, seq // STEP, body)
        put = store(rows16, image_rows(r.layer_out, b), 2)
        put.start()
        put.wait()

    feed_out(3 * images, 0)
    service(3 * images, piece, piece, fill=(lambda: units(0, 0), None))

    def backward_cross(b):
        job = 3 * images + 1 + b
        gets = [
            load(image_rows(r.after_cross, b), hid32, 0),
            load(image_rows(r.cot, b), rows16, 1),
        ]
        start_all(gets)
        settle(job - images, piece)
        wait_all(gets)

        def base(span):
            top = rows16[span, :].astype(FULL)
            sums[6:7, :] += jnp.sum(top, axis=0, keepdims=True)
            return top

        norm_backward(2, lambda span: hid32[span, :], mod(2 * images + b, slots), base, True)
        puts = [
            store(grad32, image_rows(r.grad_rows, b), 0),
            store(normed, image_rows(r.low2, b), 1),
        ]
        start_all(puts)
        d_mix[...] = dot_nt(normed[...], o_w[...]).astype(LOW)
        pulled = [
            attend_back(
                d_mix[:, head(h)],
                q2[b, :, head(h)],
                kv2[b, :, head(h)],
                kv2[b, :, head(h, 1)],
                prob2[b, h],
            )
            for h in range(heads)
        ]
        for h, (d_query, d_key, d_value) in enumerate(pulled):
            q2[b, :, head(h)] = d_query
            kv2[b, :, head(h)] = d_key
            kv2[b, :, head(h, 1)] = d_value
        slot = mod(job, images)

        def out(t):
            part[slot, :, at(t, tile)] = dot_nt(q2[b], q_w[at(t, tile), :]).astype(LOW)

        loop(0, width // tile, out)
        emit(job, piece)
        service(job, piece, piece, fill=(lambda: units(1 + b, 0), None))
        wait_all(puts)

    loop(0, images, backward_cross)

    def second_out(b):
        job = 4 * images + b
        feed_out(job, b)

        @pl.when(b == 1)
        def _():
            out_load(0).start()
            finish_out(3 * images, 0)

        service(
            job,
            piece,
            piece,
            fill=(lambda: units(2 * b - 2, 1), lambda: units(2 * b - 1, 1)),
        )

    loop(1, images, second_out)

    def backward_self(b):
        job = 5 * images + b
        gets = [
            load(image_rows(r.after_self, b), hid32, 0),
            load(image_rows(r.grad_rows, b), grad32, 1),
        ]
        start_all(gets)
        settle(job - images, piece)
        wait_all(gets)
        norm_backward(
            1,
            lambda span: hid32[span, :],
            mod(3 * images + 1 + b, slots),
            lambda span: grad32[span, :],
            True,
        )
        puts = [
            store(grad32, image_rows(r.grad_rows, b), 0),
            store(normed, image_rows(r.low1, b), 1),
        ]
        start_all(puts)
        pl.when(b > 0)(lambda: out_load(b).start())
        wait_first(b, self_weights())
        total = None
        for c in range(blocks):
            term = dot_nt(
                normed[:, pl.ds(c * cols, cols)], wide[pl.ds(c * cols, cols), pl.ds(3 * cols, cols)]
            )
            total = term if total is None else total + term
        d_mix[...] = total.astype(LOW)
        pulled = [
            attend_back(
                d_mix[:, head(h)],
                proj[b, :, head(h)],
                proj[b, :, head(h, 1)],
                proj[b, :, head(h, 2)],
                prob1[b, h],
            )
            for h in range(heads)
        ]
        for h, (d_query, d_key, d_value) in enumerate(pulled):
            proj[b, :, head(h)] = d_query
            proj[b, :, head(h, 1)] = d_key
            proj[b, :, head(h, 2)] = d_value
        slot = mod(job, images)

        def out(t):
            part[slot, :, at(t, tile)] = dot_nt(
                proj[b], wide[at(t, tile), pl.ds(0, 3 * cols)]
            ).astype(LOW)

        loop(0, width // tile, out)
        emit(job, piece)
        wait_all(puts)

        def fill(half_of):
            pl.when(b < 2)(lambda: units(2 * b + half_of, 2))

            @pl.when(b == 2)
            def _():
                units(2 * half_of, 3)
                units(2 * half_of + 1, 3)

        service(job, piece, piece, fill=(lambda: fill(0), lambda: fill(1)))
        pl.when(b > 0)(lambda: finish_out(4 * images + b, b))

    loop(0, images, backward_self)

    for b in range(images):
        job = 6 * images + b
        gets = [
            load(image_rows(r.tokens, b), rows16, 0),
            load(image_rows(r.grad_rows, b), grad32, 1),
        ]
        start_all(gets)
        settle(job - images, piece)
        slot = mod(job, images)

        def out(t, slot=slot, b=b):
            part[slot, :text_rows, at(t, tile)] = dot_nt(kv2[b], kv_w[at(t, tile), :]).astype(LOW)

        loop(0, width // tile, out)
        emit(job, small)
        wait_all(gets)
        norm_backward(
            0,
            lambda span: rows16[span, :].astype(FULL),
            mod(5 * images + b, slots),
            lambda span: grad32[span, :],
            False,
        )
        put = store(grad32, image_rows(r.token_grad, b), 0)
        put.start()
        late = [
            (lambda: unit_finish(4 * chips - 1), lambda: unit_send(4 * chips - 1)),
            (None, None),
            (None, None),
        ]
        service(job, small, piece if b == 0 else small, fill=late[b])
        put.wait()

    def small_copy(hop):
        return pltpu.make_async_remote_copy(
            src_ref=sums,
            dst_ref=r.sums_in.at[member],
            send_sem=r.sum_send.at[hop],
            recv_sem=r.sum_recv.at[hop],
            device_id={"dp": lax.rem(member + hop, n_dp)},
            device_id_type=MESH,
        )

    for hop in range(1, n_dp):
        small_copy(hop).start()
    r.sums_in[member] = sums[...]

    last = 7 * images - 1
    fold(last, 2, small)
    fold(last, 3, small)
    for p in range(PIECES):
        spread(last, p, small)
    text_puts = []
    for b in range(images):
        job = 6 * images + b
        settle(job, small)
        text_puts.append(
            store(
                inbox.at[mod(job, slots), pl.ds(0, text_rows)],
                r.text_sum.at[at(b, text_rows)],
                b,
            )
        )
        text_puts[-1].start()

    wait_all(text_puts)
    for hop in range(1, n_dp):
        small_copy(hop).wait()
    whole = r.sums_in[0]
    for d in range(1, n_dp):
        whole = whole + r.sums_in[d]
    r.sums_out[...] = whole

    for q in range(4):
        for far in range(1, chips):
            chip_copy(q * chips + far - 1, q, far).wait()


class Ends(NamedTuple):
    layer_out: Any
    token_grad: Any
    text_grad: Any
    w_self: Any
    wo_self: Any
    wq: Any
    wkv: Any
    wo_cross: Any
    w_up: Any
    bias_up: Any
    w_down: Any
    bias_down: Any
    gain: Any
    shift: Any


class Held(NamedTuple):
    shares: Any
    text_low: Any
    text: Any
    token_grad: Any
    layer_out: Any
    w_self: Any
    wo_self: Any
    wq: Any
    wkv: Any
    wo_cross: Any
    w_up: Any
    w_down: Any
    load_sem: Any
    put_sem: Any


def closing_kernel(chips, cols, shares, token_grad, layer_out, text_sum, sums, *refs):
    ends = Ends(*refs[: len(Ends._fields)])
    held = Held(*refs[len(Ends._fields) :])
    parts = shares.shape[3] // cols
    text_load = pltpu.make_async_copy(text_sum, held.text_low, held.load_sem.at[4 * chips])
    loads = [
        [
            pltpu.make_async_copy(
                shares.at[q, c], held.shares.at[q, c], held.load_sem.at[q * chips + c]
            )
            for c in range(chips)
        ]
        for q in range(4)
    ]
    puts = []

    def put(src, dst):
        copy = pltpu.make_async_copy(src, dst, held.put_sem.at[len(puts)])
        copy.start()
        puts.append(copy)

    for q in range(4):
        for copy in loads[q]:
            copy.start()
    more = [
        pltpu.make_async_copy(token_grad, held.token_grad, held.load_sem.at[4 * chips + 1]),
        pltpu.make_async_copy(layer_out, held.layer_out, held.load_sem.at[4 * chips + 2]),
    ]
    for copy in more:
        copy.start()
    text_load.start()
    ends.bias_up[...] = sums[7:8, : ends.bias_up.shape[1]]
    ends.bias_down[...] = sums[6:7, :]
    ends.gain[...] = sums[0:3, :]
    ends.shift[...] = sums[3:6, :]

    def total(q, j):
        span = pl.ds(j * cols, cols)
        whole = held.shares[q, 0, :, span].astype(FULL)
        for c in range(1, chips):
            whole = whole + held.shares[q, c, :, span].astype(FULL)
        return whole

    for q in range(4):
        for copy in loads[q]:
            copy.wait()
        for j in range(parts):
            whole = total(q, j)
            if q == 0:
                held.w_down[pl.ds(j * cols, cols), :] = whole.T
            elif q == 1:
                held.w_up[:, pl.ds(j * cols, cols)] = whole
            elif j == 0:
                (held.wo_cross if q == 2 else held.wo_self)[...] = whole.T
            elif q == 3:
                held.w_self[j - 1] = whole
            elif j == 1:
                held.wq[...] = whole
            else:
                held.wkv[j - 2] = whole
        if q == 0:
            put(held.w_down, ends.w_down)
        elif q == 1:
            put(held.w_up, ends.w_up)
        elif q == 2:
            put(held.wo_cross, ends.wo_cross)
            put(held.wq, ends.wq)
            put(held.wkv, ends.wkv)
        else:
            put(held.wo_self, ends.wo_self)
            put(held.w_self, ends.w_self)
    more[0].wait()
    put(held.token_grad, ends.token_grad)
    more[1].wait()
    put(held.layer_out, ends.layer_out)
    text_load.wait()
    held.text[...] = held.text_low[...].astype(FULL)
    put(held.text, ends.text_grad)
    for copy in puts:
        copy.wait()


def local(
    n_mp,
    n_dp,
    tokens,
    text,
    text_len,
    text_mask,
    cotangent,
    w_self,
    wo_self,
    wq_cross,
    wkv_cross,
    wo_cross,
    w_up,
    bias_up,
    w_down,
    bias_down,
    ln_gain,
    ln_bias,
):
    images, seq, width = tokens.shape
    text_rows = text.shape[1]
    cols = w_self.shape[2]
    hidden = w_up.shape[1]
    heads = cols // HEAD_DIM
    rows = images * seq
    chips = n_dp // 2
    block = width // n_dp
    tile = min(512, hidden, width)

    def out(*shape, kind=LOW):
        return jax.ShapeDtypeStruct(shape, kind)

    outs = Outputs(
        layer_out=out(rows, width),
        token_grad=out(rows, width, kind=FULL),
        text_sum=out(images * text_rows, width),
        shares=out(4, chips, block, hidden),
        sums_out=out(8, width, kind=FULL),
        norm1=out(rows, width),
        norm2=out(rows, width),
        norm3=out(rows, width),
        low1=out(rows, width),
        low2=out(rows, width),
        act_all=out(rows, hidden),
        pre_all=out(rows, hidden),
        after_self=out(rows, width, kind=FULL),
        after_cross=out(rows, width, kind=FULL),
        grad_rows=out(rows, width, kind=FULL),
        staged=out(4 * chips, block, hidden),
    )
    slots = 2 * images

    def buf(*shape, kind=LOW):
        return pltpu.VMEM(shape, kind)

    dma = pltpu.SemaphoreType.DMA
    scratch = Scratch(
        wide=buf(width, hidden),
        down=buf(hidden, width),
        kv_w=buf(width, 2 * cols),
        q_w=buf(width, cols),
        o_w=buf(cols, width),
        inbox=buf(slots, seq, width),
        outbox=buf(images, seq, width),
        part=buf(images, seq, width),
        proj=buf(images, seq, 3 * cols),
        mix1=buf(images, seq, cols),
        prob1=buf(images, heads, seq, seq),
        q2=buf(images, seq, cols),
        kv2=buf(images, text_rows, 2 * cols),
        mix2=buf(images, seq, cols),
        prob2=buf(images, heads, seq, text_rows),
        hid32=buf(seq, width, kind=FULL),
        grad32=buf(seq, width, kind=FULL),
        normed=buf(seq, width),
        rows16=buf(seq, width),
        d_pre=buf(seq, hidden),
        active=buf(seq, hidden),
        d_mix=buf(seq, cols),
        tile=buf(2 * block, hidden),
        tile_sum=buf(block, hidden),
        tile_in=buf(2, block, hidden),
        unit_cols=buf(3, rows, max(tile, 2 * block)),
        x_text=buf(images * text_rows, 2 * block),
        sums=buf(8, width, kind=FULL),
        sums_in=buf(n_dp, 8, width, kind=FULL),
        send_sem=dma((images, PIECES)),
        out_sem=dma((images, PIECES)),
        in_sem=dma((slots, PIECES)),
        pass_sem=dma((slots, PIECES)),
        weight_sem=dma((3 + width // cols + 5,)),
        load_sem=dma((2,)),
        store_sem=dma((4,)),
        unit_sem=dma((6,)),
        core_send=dma((4 * chips,)),
        core_recv=dma((4 * chips,)),
        chip_send=dma((4 * chips,)),
        chip_recv=dma((4, chips)),
        sum_send=dma((n_dp,)),
        sum_recv=dma((n_dp,)),
    )
    vmem = pl.BlockSpec(memory_space=pltpu.VMEM)
    anywhere = pl.BlockSpec(memory_space=pl.ANY)
    sizes = (n_mp, n_dp, images, seq, width, text_rows, cols, hidden)
    results = pl.pallas_call(
        functools.partial(layer_kernel, sizes),
        out_shape=tuple(outs),
        in_specs=list(
            Inputs(*[anywhere] * len(Inputs._fields))._replace(
                length=vmem, kept=vmem, bias_up=vmem, bias_down=vmem, gain=vmem, shift=vmem
            )
        ),
        out_specs=tuple(Outputs(*[anywhere] * len(outs))._replace(sums_out=vmem)),
        scratch_shapes=list(scratch),
        compiler_params=pltpu.CompilerParams(
            collective_id=0, has_side_effects=True, vmem_limit_bytes=VMEM_LIMIT
        ),
        name="layer",
    )(
        tokens.reshape(rows, width),
        text.reshape(images * text_rows, width),
        text_len.reshape(1, images),
        text_mask,
        cotangent.reshape(rows, width),
        w_self,
        wo_self,
        wq_cross,
        wkv_cross,
        wo_cross,
        w_up,
        bias_up.reshape(1, hidden),
        w_down,
        bias_down.reshape(1, width),
        ln_gain,
        ln_bias,
    )
    got = Outputs(*results)
    shapes = Ends(
        layer_out=out(rows, width),
        token_grad=out(rows, width, kind=FULL),
        text_grad=out(images * text_rows, width, kind=FULL),
        w_self=out(3, block, cols, kind=FULL),
        wo_self=out(cols, block, kind=FULL),
        wq=out(block, cols, kind=FULL),
        wkv=out(2, block, cols, kind=FULL),
        wo_cross=out(cols, block, kind=FULL),
        w_up=out(block, hidden, kind=FULL),
        bias_up=out(1, hidden, kind=FULL),
        w_down=out(hidden, block, kind=FULL),
        bias_down=out(1, width, kind=FULL),
        gain=out(3, width, kind=FULL),
        shift=out(3, width, kind=FULL),
    )
    staging = Held(
        shares=buf(4, chips, block, hidden),
        text_low=buf(images * text_rows, width),
        text=buf(images * text_rows, width, kind=FULL),
        token_grad=buf(rows, width, kind=FULL),
        layer_out=buf(rows, width),
        w_self=buf(3, block, cols, kind=FULL),
        wo_self=buf(cols, block, kind=FULL),
        wq=buf(block, cols, kind=FULL),
        wkv=buf(2, block, cols, kind=FULL),
        wo_cross=buf(cols, block, kind=FULL),
        w_up=buf(block, hidden, kind=FULL),
        w_down=buf(hidden, block, kind=FULL),
        load_sem=dma((4 * chips + 3,)),
        put_sem=dma((10,)),
    )
    ends = Ends(
        *pl.pallas_call(
            functools.partial(closing_kernel, chips, cols),
            out_shape=tuple(shapes),
            in_specs=[anywhere] * 4 + [vmem],
            out_specs=tuple(
                Ends(*[anywhere] * len(shapes))._replace(
                    bias_up=vmem, bias_down=vmem, gain=vmem, shift=vmem
                )
            ),
            scratch_shapes=list(staging),
            compiler_params=pltpu.CompilerParams(vmem_limit_bytes=VMEM_LIMIT),
            name="closing",
        )(got.shares, got.token_grad, got.layer_out, got.text_sum, got.sums_out)
    )
    return (
        ends.layer_out.reshape(images, seq, width),
        ends.token_grad.reshape(images, seq, width),
        ends.text_grad.reshape(images, text_rows, width),
        ends.w_self,
        ends.wo_self,
        ends.wq,
        ends.wkv,
        ends.wo_cross,
        ends.w_up,
        ends.bias_up.reshape(hidden),
        ends.w_down,
        ends.bias_down.reshape(width),
        ends.gain,
        ends.shift,
    )


def solution(mesh):
    placed = (
        P("dp", None, None),
        P("dp", None, None),
        P("dp"),
        P("dp", None),
        P("dp", None, None),
        P(None, None, "mp"),
        P("mp", None),
        P(None, "mp"),
        P(None, None, "mp"),
        P("mp", None),
        P(None, "mp"),
        P("mp"),
        P("mp", None),
        P(),
        P(),
        P(),
    )
    return jax.shard_map(
        functools.partial(local, mesh.shape["mp"], mesh.shape["dp"]),
        mesh=mesh,
        in_specs=placed,
        out_specs=(
            P("dp", None, None),
            P("dp", None, None),
            P("dp", None, None),
            P(None, "dp", "mp"),
            P("mp", "dp"),
            P("dp", "mp"),
            P(None, "dp", "mp"),
            P("mp", "dp"),
            P("dp", "mp"),
            P("mp"),
            P("mp", "dp"),
            P(),
            P(),
            P(),
        ),
        check_vma=False,
    )
```

```python
import functools
from typing import Any, NamedTuple

import jax
import jax.numpy as jnp
from jax import lax
from jax.experimental import pallas as pl
from jax.experimental.pallas import tpu as pltpu
from jax.sharding import PartitionSpec as P

HEAD_DIM = 128
MASKED = -1e30
NORM_EPS = 1e-05
PIECES = 4
STEP = 64
LOW = jnp.bfloat16
FULL = jnp.float32
MESH = pl.DeviceIdType.MESH
VMEM_LIMIT = 64 * 1024 * 1024 - 512 * 1024

class Inputs(NamedTuple):
    tokens: Any
    text: Any
    length: Any
    kept: Any
    cot: Any
    w_self: Any
    wo_self: Any
    wq: Any
    wkv: Any
    wo_cross: Any
    w_up: Any
    bias_up: Any
    w_down: Any
    bias_down: Any
    gain: Any
    shift: Any


class Outputs(NamedTuple):
    layer_out: Any
    token_grad: Any
    text_sum: Any
    shares: Any
    sums_out: Any
    norm1: Any
    norm2: Any
    norm3: Any
    low1: Any
    low2: Any
    act_all: Any
    pre_all: Any
    after_self: Any
    after_cross: Any
    grad_rows: Any
    staged: Any


class Scratch(NamedTuple):
    wide: Any
    down: Any
    kv_w: Any
    q_w: Any
    o_w: Any
    inbox: Any
    outbox: Any
    part: Any
    proj: Any
    mix1: Any
    prob1: Any
    q2: Any
    kv2: Any
    mix2: Any
    prob2: Any
    hid32: Any
    grad32: Any
    normed: Any
    rows16: Any
    d_pre: Any
    active: Any
    d_mix: Any
    tile: Any
    tile_sum: Any
    tile_in: Any
    unit_cols: Any
    x_text: Any
    sums: Any
    sums_in: Any
    send_sem: Any
    out_sem: Any
    in_sem: Any
    pass_sem: Any
    weight_sem: Any
    load_sem: Any
    store_sem: Any
    unit_sem: Any
    core_send: Any
    core_recv: Any
    chip_send: Any
    chip_recv: Any
    sum_send: Any
    sum_recv: Any


class Refs(NamedTuple):
    tokens: Any
    text: Any
    length: Any
    kept: Any
    cot: Any
    w_self: Any
    wo_self: Any
    wq: Any
    wkv: Any
    wo_cross: Any
    w_up: Any
    bias_up: Any
    w_down: Any
    bias_down: Any
    gain: Any
    shift: Any
    layer_out: Any
    token_grad: Any
    text_sum: Any
    shares: Any
    sums_out: Any
    norm1: Any
    norm2: Any
    norm3: Any
    low1: Any
    low2: Any
    act_all: Any
    pre_all: Any
    after_self: Any
    after_cross: Any
    grad_rows: Any
    staged: Any
    wide: Any
    down: Any
    kv_w: Any
    q_w: Any
    o_w: Any
    inbox: Any
    outbox: Any
    part: Any
    proj: Any
    mix1: Any
    prob1: Any
    q2: Any
    kv2: Any
    mix2: Any
    prob2: Any
    hid32: Any
    grad32: Any
    normed: Any
    rows16: Any
    d_pre: Any
    active: Any
    d_mix: Any
    tile: Any
    tile_sum: Any
    tile_in: Any
    unit_cols: Any
    x_text: Any
    sums: Any
    sums_in: Any
    send_sem: Any
    out_sem: Any
    in_sem: Any
    pass_sem: Any
    weight_sem: Any
    load_sem: Any
    store_sem: Any
    unit_sem: Any
    core_send: Any
    core_recv: Any
    chip_send: Any
    chip_recv: Any
    sum_send: Any
    sum_recv: Any


def dot_nn(left, right):
    return jnp.dot(left, right, preferred_element_type=FULL)


def dot_nt(left, right):
    return lax.dot_general(left, right, (((1,), (1,)), ((), ())), preferred_element_type=FULL)


def dot_tn(left, right):
    return lax.dot_general(left, right, (((0,), (0,)), ((), ())), preferred_element_type=FULL)


def mod(value, size):
    return value % size if isinstance(value, int) else lax.rem(value, size)


def at(index, size):
    return pl.ds(pl.multiple_of(index * size, size), size)


def loop(start, stop, body):
    def step(index, carry):
        body(index)
        return carry

    lax.fori_loop(start, stop, step, 0)


def layer_kernel(sizes, *refs):
    r = Refs(*refs)
    n_mp, n_dp, images, seq, width, text_rows, cols, hidden = sizes
    heads = cols // HEAD_DIM
    scale = HEAD_DIM**-0.5
    half = n_mp // 2
    slots = 2 * images
    piece = seq // PIECES
    small = text_rows // PIECES
    chips = n_dp // 2
    block = width // n_dp
    tile = min(512, hidden, width)
    wide, down, kv_w, q_w, o_w = r.wide, r.down, r.kv_w, r.q_w, r.o_w
    inbox, outbox, part = r.inbox, r.outbox, r.part
    hid32, grad32, normed, rows16 = r.hid32, r.grad32, r.normed, r.rows16
    proj, mix1, prob1, q2, kv2 = r.proj, r.mix1, r.prob1, r.q2, r.kv2
    mix2, prob2, d_pre, active, d_mix = r.mix2, r.prob2, r.d_pre, r.active, r.d_mix
    sums = r.sums
    place = lax.axis_index("mp")
    member = lax.axis_index("dp")
    core = lax.rem(member, 2)
    chip = lax.div(member, 2)
    low_half = place < half
    at_end = (place == 0) | (place == n_mp - 1)
    not_end = jnp.logical_not(at_end)
    at_mid = (place == half - 1) | (place == half)
    inner = jnp.where(low_half, place + 1, place - 1)
    outer = jnp.where(at_end, place, jnp.where(low_half, place - 1, place + 1))

    def load(src, dst, index):
        return pltpu.make_async_copy(src, dst, r.load_sem.at[index])

    def store(src, dst, index):
        return pltpu.make_async_copy(src, dst, r.store_sem.at[index])

    blocks = width // cols

    def self_weights():
        made = [
            pltpu.make_async_copy(
                r.w_self.at[j], wide.at[:, pl.ds(j * cols, cols)], r.weight_sem.at[j]
            )
            for j in range(3)
        ]
        for c in range(blocks):
            made.append(
                pltpu.make_async_copy(
                    r.wo_self.at[:, pl.ds(c * cols, cols)],
                    wide.at[pl.ds(c * cols, cols), pl.ds(3 * cols, cols)],
                    r.weight_sem.at[3 + c],
                )
            )
        return made

    other = 3 + blocks

    def up_weights():
        return [pltpu.make_async_copy(r.w_up, wide, r.weight_sem.at[0])]

    def down_weights():
        return [pltpu.make_async_copy(r.w_down, down, r.weight_sem.at[other])]

    def kv_weights():
        return [
            pltpu.make_async_copy(
                r.wkv.at[j], kv_w.at[:, pl.ds(j * cols, cols)], r.weight_sem.at[other + 1 + j]
            )
            for j in range(2)
        ]

    def cross_weights():
        return [
            pltpu.make_async_copy(r.wq, q_w, r.weight_sem.at[other + 3]),
            pltpu.make_async_copy(r.wo_cross, o_w, r.weight_sem.at[other + 4]),
        ]

    def start_all(copies):
        for copy in copies:
            copy.start()

    def wait_all(copies):
        for copy in copies:
            copy.wait()

    def wait_first(index, copies):
        @pl.when(index == 0)
        def _():
            wait_all(copies)

    def sum_copy(job, p, rows, swap):
        span = pl.ds(p * rows, rows)
        slot, deep = mod(job, images), mod(job, slots)
        return pltpu.make_async_remote_copy(
            src_ref=part.at[slot, span],
            dst_ref=inbox.at[deep, span] if swap else outbox.at[slot, span],
            send_sem=r.send_sem.at[slot, p],
            recv_sem=r.in_sem.at[deep, p] if swap else r.out_sem.at[slot, p],
            device_id={"mp": inner},
            device_id_type=MESH,
        )

    def pass_copy(job, p, rows):
        span = pl.ds(p * rows, rows)
        deep = mod(job, slots)
        return pltpu.make_async_remote_copy(
            src_ref=inbox.at[deep, span],
            dst_ref=inbox.at[deep, span],
            send_sem=r.pass_sem.at[deep, p],
            recv_sem=r.in_sem.at[deep, p],
            device_id={"mp": outer},
            device_id_type=MESH,
        )

    def emit(job, rows):
        @pl.when(at_end)
        def _():
            for p in range(PIECES):
                sum_copy(job, p, rows, half == 1).start()

    def fold(job, p, rows):
        if half == 1:
            return
        span = pl.ds(p * rows, rows)
        slot = mod(job, images)

        @pl.when(not_end)
        def _():
            sum_copy(job, p, rows, False).wait_recv()
            part[slot, span] = part[slot, span] + outbox[slot, span]

        @pl.when(at_mid)
        def _():
            sum_copy(job, p, rows, True).start()

        if half > 2:

            @pl.when(jnp.logical_not(at_mid | at_end))
            def _():
                sum_copy(job, p, rows, False).start()

    def spread(job, p, rows):
        span = pl.ds(p * rows, rows)
        slot, deep = mod(job, images), mod(job, slots)

        @pl.when(at_mid)
        def _():
            pass_copy(job, p, rows).wait_recv()
            inbox[deep, span] = part[slot, span] + inbox[deep, span]

        if half > 2:

            @pl.when(jnp.logical_not(at_mid | at_end))
            def _():
                pass_copy(job, p, rows).wait_recv()

        if half > 1:

            @pl.when(not_end)
            def _():
                pass_copy(job, p, rows).start()

    def settle(job, rows):
        for p in range(PIECES):
            sum_copy(job, p, rows, False).wait_send()
        if half > 1:

            @pl.when(not_end)
            def _():
                for p in range(PIECES):
                    pass_copy(job, p, rows).wait_send()

            @pl.when(at_end)
            def _():
                for p in range(PIECES):
                    pass_copy(job, p, rows).wait_recv()

    def service(job, rows, before, first=False, fill=(None, None)):
        def run(body):
            if first:
                pl.when(job > 0)(body)
            else:
                body()

        @run
        def _():
            fold(job - 1, 2, before)
            fold(job - 1, 3, before)
            spread(job - 1, 0, before)
            spread(job - 1, 1, before)

        if fill[0]:
            fill[0]()
        fold(job, 0, rows)

        @run
        def _():
            spread(job - 1, 2, before)

        if fill[1]:
            fill[1]()
        fold(job, 1, rows)

        @run
        def _():
            spread(job - 1, 3, before)

    def norm_stats(x):
        mean = jnp.mean(x, axis=-1, keepdims=True)
        centred = x - mean
        var = jnp.mean(centred * centred, axis=-1, keepdims=True)
        inv = lax.rsqrt(var + NORM_EPS)
        return centred * inv, inv

    def norm_forward(which, read, keep):
        def body(i):
            span = at(i, STEP)
            x = read(span)
            unit, _ = norm_stats(x)
            if keep:
                hid32[span, :] = x
            normed[span, :] = (
                unit * r.gain[which : which + 1, :] + r.shift[which : which + 1, :]
            ).astype(LOW)

        loop(0, seq // STEP, body)

    def norm_backward(which, read, deep, base, low):
        def body(i):
            span = at(i, STEP)
            unit, inv = norm_stats(read(span))
            grad = inbox[deep, span].astype(FULL)
            sums[which : which + 1, :] += jnp.sum(grad * unit, axis=0, keepdims=True)
            sums[3 + which : 4 + which, :] += jnp.sum(grad, axis=0, keepdims=True)
            scaled = grad * r.gain[which : which + 1, :]
            back = inv * (
                scaled
                - jnp.mean(scaled, axis=-1, keepdims=True)
                - unit * jnp.mean(scaled * unit, axis=-1, keepdims=True)
            )
            whole = base(span) + back
            grad32[span, :] = whole
            if low:
                normed[span, :] = whole.astype(LOW)

        loop(0, seq // STEP, body)

    def attend(queries, keys, values, valid):
        scores = dot_nt(queries, keys) * scale
        if valid is not None:
            scores = jnp.where(valid, scores, MASKED)
        powers = jnp.exp(scores - jnp.max(scores, axis=-1, keepdims=True))
        weight = (powers / jnp.sum(powers, axis=-1, keepdims=True)).astype(LOW)
        return dot_nn(weight, values).astype(LOW), weight

    def attend_back(d_out, queries, keys, values, weight):
        prob = weight.astype(FULL)
        d_weight = dot_nt(d_out, values)
        d_value = dot_tn(weight, d_out)
        d_score = (
            prob * (d_weight - jnp.sum(d_weight * prob, axis=-1, keepdims=True))
        ).astype(LOW)
        d_query = dot_nn(d_score, keys) * scale
        d_key = dot_tn(d_score, queries) * scale
        return d_query.astype(LOW), d_key.astype(LOW), d_value.astype(LOW)

    def head(h, group=0):
        return pl.ds(group * cols + h * HEAD_DIM, HEAD_DIM)

    def chip_at(far):
        down_y = lax.rem(lax.div(chip, 2) + far // 2, chips // 2)
        return 2 * down_y + lax.rem(lax.rem(chip, 2) + far % 2, 2)

    def core_copy(turn):
        return pltpu.make_async_remote_copy(
            src_ref=r.tile.at[at(1 - core, block)],
            dst_ref=r.tile_in.at[mod(turn, 2)],
            send_sem=r.core_send.at[turn],
            recv_sem=r.core_recv.at[turn],
            device_id={"dp": member + 1 - 2 * core},
            device_id_type=MESH,
        )

    def chip_copy(turn, q, far):
        return pltpu.make_async_remote_copy(
            src_ref=r.staged.at[turn],
            dst_ref=r.shares.at[q, far],
            send_sem=r.chip_send.at[turn],
            recv_sem=r.chip_recv.at[q, far],
            device_id={"dp": 2 * chip_at(far) + core},
            device_id_type=MESH,
        )

    def unit_finish(turn):
        q, i = lax.div(turn, chips), lax.rem(turn, chips)
        slot = lax.rem(turn, 2)
        core_copy(turn).wait()

        def body(k):
            span = at(k, STEP)
            own = pl.ds(pl.multiple_of(core * block + k * STEP, STEP), STEP)
            r.tile_sum[span, :] = r.tile[own, :] + r.tile_in[slot, span]

        loop(0, block // STEP, body)

        @pl.when(i == chips - 1)
        def _():
            pltpu.make_async_copy(r.tile_sum, r.shares.at[q, 0], r.unit_sem.at[5]).start()

        @pl.when(i < chips - 1)
        def _():
            pltpu.make_async_copy(r.tile_sum, r.staged.at[turn], r.unit_sem.at[5]).start()

    def unit_send(turn):
        q, i = lax.div(turn, chips), lax.rem(turn, chips)
        pltpu.make_async_copy(r.tile_sum, r.staged.at[turn], r.unit_sem.at[5]).wait()

        @pl.when(i < chips - 1)
        def _():
            chip_copy(turn, q, i + 1).start()

    rows_all = images * seq
    text_all = images * text_rows

    def unit(q, i):
        turn = q * chips + i
        target = chip_at(mod(i + 1, chips))

        def x_load(which, src):
            return pltpu.make_async_copy(
                src.at[:, at(target, 2 * block)],
                r.x_text if which == 2 else r.unit_cols.at[which, :, pl.ds(0, 2 * block)],
                r.unit_sem.at[which],
            )

        def y_load(src, t):
            return pltpu.make_async_copy(
                src.at[:, pl.ds(t * tile, tile)],
                r.unit_cols.at[1 + t % 2, :, pl.ds(0, tile)],
                r.unit_sem.at[3 + t % 2],
            )

        def held(ref, rows, start):
            return ref[:, :, pl.ds(start, cols)].reshape(rows, cols)

        if q < 2:
            xs = [x_load(0, r.norm3 if q else r.cot)]
            ys = [y_load(r.pre_all if q else r.act_all, t) for t in range(hidden // tile)]
            start_all(ys[:2])
        elif q == 2:
            xs = [x_load(0, r.low2), x_load(1, r.norm2), x_load(2, r.text)]
        else:
            xs = [x_load(0, r.low1), x_load(1, r.norm1)]
        start_all(xs)

        @pl.when(turn > 0)
        def _():
            unit_finish(turn - 1)

        wait_all(xs)

        def turned(which):
            return r.unit_cols[which, :, : 2 * block].T

        def put(offset, left, right):
            r.tile[:, pl.ds(offset, right.shape[1])] = dot_nn(left, right).astype(LOW)

        if q < 2:
            left = turned(0)
            for t, copy in enumerate(ys):
                copy.wait()
                put(t * tile, left, r.unit_cols[1 + t % 2, :, :tile])
                if t + 2 < len(ys):
                    ys[t + 2].start()
        elif q == 2:
            put(0, turned(0), held(mix2, rows_all, 0))
            put(cols, turned(1), held(q2, rows_all, 0))
            left = r.x_text[...].T
            for j in range(2):
                put((2 + j) * cols, left, held(kv2, text_all, j * cols))
        else:
            put(0, turned(0), held(mix1, rows_all, 0))
            left = turned(1)
            for j in range(3):
                put((1 + j) * cols, left, held(proj, rows_all, j * cols))
        core_copy(turn).start()

        @pl.when(turn > 0)
        def _():
            unit_send(turn - 1)

    quarter = chips // 4

    def units(b, q):
        loop(b * quarter, (b + 1) * quarter, functools.partial(unit, q))

    first_rows = load(r.tokens.at[pl.ds(0, seq)], rows16, 0)
    first_rows.start()
    start_all(self_weights())
    sums[...] = jnp.zeros_like(sums)

    barrier = pltpu.get_barrier_semaphore()
    for hop in range(1, n_dp):
        pl.semaphore_signal(
            barrier, inc=1, device_id={"dp": lax.rem(member + hop, n_dp)}, device_id_type=MESH
        )
    pl.semaphore_signal(barrier, inc=1, device_id={"mp": inner}, device_id_type=MESH)
    if half > 1:

        @pl.when(not_end)
        def _():
            pl.semaphore_signal(barrier, inc=1, device_id={"mp": outer}, device_id_type=MESH)
            pl.semaphore_wait(barrier, n_dp + 1)

        @pl.when(at_end)
        def _():
            pl.semaphore_wait(barrier, n_dp)
    else:
        pl.semaphore_wait(barrier, n_dp)


    def image_rows(ref, b):
        return ref.at[at(b, seq)]

    def forward_self(b):
        load(image_rows(r.tokens, b), rows16, 0).wait()
        norm_forward(0, lambda span: rows16[span, :].astype(FULL), False)
        put = store(normed, image_rows(r.norm1, b), 0)
        put.start()
        wait_first(b, self_weights())

        @pl.when(b == 0)
        def _():
            start_all(kv_weights() + cross_weights() + down_weights())

        def project(j):
            proj[b, :, at(j, cols)] = dot_nn(normed[...], wide[:, at(j, cols)]).astype(LOW)

        loop(0, 3, project)
        made = [
            attend(proj[b, :, head(h)], proj[b, :, head(h, 1)], proj[b, :, head(h, 2)], None)
            for h in range(heads)
        ]
        for h, (mixed, weight) in enumerate(made):
            mix1[b, :, head(h)] = mixed
            prob1[b, h] = weight

        def out(c):
            part[b, :, at(c, cols)] = dot_nn(
                mix1[b], wide[at(c, cols), pl.ds(3 * cols, cols)]
            ).astype(LOW)

        loop(0, blocks, out)
        emit(b, piece)
        get = load(r.text.at[at(b, text_rows)], rows16.at[pl.ds(0, text_rows)], 0)
        get.start()

        def text_side():
            get.wait()
            wait_first(b, kv_weights())

            def key_value(j):
                kv2[b, :, at(j, cols)] = dot_nn(
                    rows16[pl.ds(0, text_rows), :], kv_w[:, at(j, cols)]
                ).astype(LOW)

            loop(0, 2, key_value)

        service(b, piece, piece, first=True, fill=(text_side, None))
        put.wait()
        pl.when(b + 1 < images)(lambda: load(image_rows(r.tokens, b + 1), rows16, 0).start())

    loop(0, images, forward_self)
    start_all(up_weights())

    def forward_cross(b):
        job = images + b
        get = load(image_rows(r.tokens, b), rows16, 0)
        get.start()
        settle(job - images, piece)
        get.wait()
        deep = mod(job - images, slots)
        norm_forward(
            1, lambda span: rows16[span, :].astype(FULL) + inbox[deep, span].astype(FULL), True
        )
        puts = [
            store(hid32, image_rows(r.after_self, b), 0),
            store(normed, image_rows(r.norm2, b), 1),
        ]
        start_all(puts)
        wait_first(b, cross_weights())
        q2[b] = dot_nn(normed[...], q_w[...]).astype(LOW)
        slot_at = lax.broadcasted_iota(jnp.int32, (1, text_rows), 1)
        image_at = lax.broadcasted_iota(jnp.int32, (1, images), 1)
        length = jnp.sum(
            jnp.where(image_at == b, r.length[...], 0), axis=1, keepdims=True, dtype=jnp.int32
        )
        valid = (slot_at < length) & (r.kept[pl.ds(b, 1), :] == 1)
        made = [
            attend(q2[b, :, head(h)], kv2[b, :, head(h)], kv2[b, :, head(h, 1)], valid)
            for h in range(heads)
        ]
        for h, (mixed, weight) in enumerate(made):
            mix2[b, :, head(h)] = mixed
            prob2[b, h] = weight

        def out(t):
            part[b, :, at(t, tile)] = dot_nn(mix2[b], o_w[:, at(t, tile)]).astype(LOW)

        loop(0, width // tile, out)
        emit(job, piece)
        service(job, piece, piece)
        wait_all(puts)

    loop(0, images, forward_cross)

    def feed_forward(b):
        job = 2 * images + b
        gets = [
            load(image_rows(r.after_self, b), hid32, 0),
            load(image_rows(r.cot, b), rows16, 1),
        ]
        start_all(gets)
        settle(job - images, piece)
        wait_all(gets)
        deep = mod(job - images, slots)
        norm_forward(2, lambda span: hid32[span, :] + inbox[deep, span].astype(FULL), True)
        puts = [
            store(hid32, image_rows(r.after_cross, b), 0),
            store(normed, image_rows(r.norm3, b), 1),
        ]
        start_all(puts)
        wait_first(b, up_weights() + down_weights())

        def middle(t):
            span = at(t, tile)
            pre = dot_nn(normed[...], wide[:, span]) + r.bias_up[:, span]
            curve = 0.5 * (1.0 + lax.erf(pre * 0.7071067811865476))
            active[:, span] = (pre * curve).astype(LOW)
            slope = curve + pre * jnp.exp(-0.5 * pre * pre) * 0.3989422804014327
            d_active = dot_nt(rows16[...], down[span, :]).astype(LOW).astype(FULL)
            d_low = (d_active * slope).astype(LOW)
            d_pre[:, span] = d_low
            sums[7:8, span] += jnp.sum(d_low.astype(FULL), axis=0, keepdims=True)

        loop(0, hidden // tile, middle)
        more = [
            store(active, image_rows(r.act_all, b), 2),
            store(d_pre, image_rows(r.pre_all, b), 3),
        ]
        start_all(more)

        def back(t):
            part[b, :, at(t, tile)] = dot_nt(d_pre[...], wide[at(t, tile), :]).astype(LOW)

        loop(0, width // tile, back)
        emit(job, piece)
        service(job, piece, piece)
        wait_all(puts + more)

    loop(0, images, feed_forward)
    start_all(self_weights())

    def feed_out(job, b):
        get = load(image_rows(r.act_all, b), active, 0)
        get.start()
        settle(job - images, piece)
        get.wait()
        slot = mod(job, images)

        def out(t):
            part[slot, :, at(t, tile)] = dot_nn(active[...], down[:, at(t, tile)]).astype(LOW)

        loop(0, width // tile, out)
        emit(job, piece)

    def out_load(b):
        return load(image_rows(r.after_cross, b), hid32, 2)

    def finish_out(job, b):
        out_load(b).wait()
        deep = mod(job, slots)

        def body(i):
            span = at(i, STEP)
            normed[span, :] = (
                hid32[span, :] + inbox[deep, span].astype(FULL) + r.bias_down[...]
            ).astype(LOW)

        loop(0, seq // STEP, body)
        put = store(normed, image_rows(r.layer_out, b), 2)
        put.start()
        put.wait()

    feed_out(3 * images, 0)
    service(3 * images, piece, piece, fill=(lambda: units(0, 0), None))

    def backward_cross(b):
        job = 3 * images + 1 + b
        gets = [
            load(image_rows(r.after_cross, b), hid32, 0),
            load(image_rows(r.cot, b), rows16, 1),
        ]
        start_all(gets)
        settle(job - images, piece)
        wait_all(gets)

        def base(span):
            top = rows16[span, :].astype(FULL)
            sums[6:7, :] += jnp.sum(top, axis=0, keepdims=True)
            return top

        norm_backward(2, lambda span: hid32[span, :], mod(2 * images + b, slots), base, True)
        puts = [
            store(grad32, image_rows(r.grad_rows, b), 0),
            store(normed, image_rows(r.low2, b), 1),
        ]
        start_all(puts)
        d_mix[...] = dot_nt(normed[...], o_w[...]).astype(LOW)
        pulled = [
            attend_back(
                d_mix[:, head(h)],
                q2[b, :, head(h)],
                kv2[b, :, head(h)],
                kv2[b, :, head(h, 1)],
                prob2[b, h],
            )
            for h in range(heads)
        ]
        for h, (d_query, d_key, d_value) in enumerate(pulled):
            q2[b, :, head(h)] = d_query
            kv2[b, :, head(h)] = d_key
            kv2[b, :, head(h, 1)] = d_value
        slot = mod(job, images)

        def out(t):
            part[slot, :, at(t, tile)] = dot_nt(q2[b], q_w[at(t, tile), :]).astype(LOW)

        loop(0, width // tile, out)
        emit(job, piece)
        service(job, piece, piece, fill=(lambda: units(1 + b, 0), None))
        wait_all(puts)

    loop(0, images, backward_cross)

    def second_out(b):
        job = 4 * images + b
        feed_out(job, b)

        @pl.when(b == 1)
        def _():
            out_load(0).start()
            finish_out(3 * images, 0)

        service(
            job,
            piece,
            piece,
            fill=(lambda: units(2 * b - 2, 1), lambda: units(2 * b - 1, 1)),
        )

    loop(1, images, second_out)

    def backward_self(b):
        job = 5 * images + b
        gets = [
            load(image_rows(r.after_self, b), hid32, 0),
            load(image_rows(r.grad_rows, b), grad32, 1),
        ]
        start_all(gets)
        settle(job - images, piece)
        wait_all(gets)
        norm_backward(
            1,
            lambda span: hid32[span, :],
            mod(3 * images + 1 + b, slots),
            lambda span: grad32[span, :],
            True,
        )
        puts = [
            store(grad32, image_rows(r.grad_rows, b), 0),
            store(normed, image_rows(r.low1, b), 1),
        ]
        start_all(puts)
        wait_first(b, self_weights())
        total = None
        for c in range(blocks):
            term = dot_nt(
                normed[:, pl.ds(c * cols, cols)], wide[pl.ds(c * cols, cols), pl.ds(3 * cols, cols)]
            )
            total = term if total is None else total + term
        d_mix[...] = total.astype(LOW)
        pulled = [
            attend_back(
                d_mix[:, head(h)],
                proj[b, :, head(h)],
                proj[b, :, head(h, 1)],
                proj[b, :, head(h, 2)],
                prob1[b, h],
            )
            for h in range(heads)
        ]
        for h, (d_query, d_key, d_value) in enumerate(pulled):
            proj[b, :, head(h)] = d_query
            proj[b, :, head(h, 1)] = d_key
            proj[b, :, head(h, 2)] = d_value
        slot = mod(job, images)

        def out(t):
            part[slot, :, at(t, tile)] = dot_nt(
                proj[b], wide[at(t, tile), pl.ds(0, 3 * cols)]
            ).astype(LOW)

        loop(0, width // tile, out)
        emit(job, piece)
        wait_all(puts)

        def fill(half_of):
            pl.when(b < 2)(lambda: units(2 * b + half_of, 2))

            @pl.when(b == 2)
            def _():
                units(2 * half_of, 3)
                if half_of == 0:
                    units(1, 3)

        service(job, piece, piece, fill=(lambda: fill(0), lambda: fill(1)))

    loop(0, images, backward_self)

    for b in range(images):
        job = 6 * images + b
        gets = [
            load(image_rows(r.tokens, b), rows16, 0),
            load(image_rows(r.grad_rows, b), grad32, 1),
        ]
        start_all(gets)
        if b + 1 < images:
            out_load(b + 1).start()
        settle(job - images, piece)
        slot = mod(job, images)

        def out(t, slot=slot, b=b):
            part[slot, :text_rows, at(t, tile)] = dot_nt(kv2[b], kv_w[at(t, tile), :]).astype(LOW)

        loop(0, width // tile, out)
        emit(job, small)
        wait_all(gets)
        norm_backward(
            0,
            lambda span: rows16[span, :].astype(FULL),
            mod(5 * images + b, slots),
            lambda span: grad32[span, :],
            False,
        )
        put = store(grad32, image_rows(r.token_grad, b), 0)
        put.start()
        if b + 1 < images:
            finish_out(4 * images + b + 1, b + 1)
        late = [
            (lambda: units(3, 3), None),
            (lambda: unit_finish(4 * chips - 1), lambda: unit_send(4 * chips - 1)),
            (None, None),
        ]
        service(job, small, piece if b == 0 else small, fill=late[b])
        put.wait()

    def small_copy(hop):
        return pltpu.make_async_remote_copy(
            src_ref=sums,
            dst_ref=r.sums_in.at[member],
            send_sem=r.sum_send.at[hop],
            recv_sem=r.sum_recv.at[hop],
            device_id={"dp": lax.rem(member + hop, n_dp)},
            device_id_type=MESH,
        )

    for hop in range(1, n_dp):
        small_copy(hop).start()
    r.sums_in[member] = sums[...]

    last = 7 * images - 1
    fold(last, 2, small)
    fold(last, 3, small)
    for p in range(PIECES):
        spread(last, p, small)
    text_puts = []
    for b in range(images):
        job = 6 * images + b
        settle(job, small)
        text_puts.append(
            store(
                inbox.at[mod(job, slots), pl.ds(0, text_rows)],
                r.text_sum.at[at(b, text_rows)],
                b,
            )
        )
        text_puts[-1].start()

    wait_all(text_puts)
    for hop in range(1, n_dp):
        small_copy(hop).wait()
    whole = r.sums_in[0]
    for d in range(1, n_dp):
        whole = whole + r.sums_in[d]
    r.sums_out[...] = whole

    for q in range(4):
        for far in range(1, chips):
            chip_copy(q * chips + far - 1, q, far).wait()


class Ends(NamedTuple):
    layer_out: Any
    token_grad: Any
    text_grad: Any
    w_self: Any
    wo_self: Any
    wq: Any
    wkv: Any
    wo_cross: Any
    w_up: Any
    bias_up: Any
    w_down: Any
    bias_down: Any
    gain: Any
    shift: Any


class Held(NamedTuple):
    shares: Any
    text_low: Any
    text: Any
    token_grad: Any
    layer_out: Any
    w_self: Any
    wo_self: Any
    wq: Any
    wkv: Any
    wo_cross: Any
    w_up: Any
    w_down: Any
    load_sem: Any
    put_sem: Any


def closing_kernel(chips, cols, shares, token_grad, layer_out, text_sum, sums, *refs):
    ends = Ends(*refs[: len(Ends._fields)])
    held = Held(*refs[len(Ends._fields) :])
    parts = shares.shape[3] // cols
    text_load = pltpu.make_async_copy(text_sum, held.text_low, held.load_sem.at[4 * chips])
    loads = [
        [
            pltpu.make_async_copy(
                shares.at[q, c], held.shares.at[q, c], held.load_sem.at[q * chips + c]
            )
            for c in range(chips)
        ]
        for q in range(4)
    ]
    puts = []

    def put(src, dst):
        copy = pltpu.make_async_copy(src, dst, held.put_sem.at[len(puts)])
        copy.start()
        puts.append(copy)

    for q in range(4):
        for copy in loads[q]:
            copy.start()
    more = [
        pltpu.make_async_copy(token_grad, held.token_grad, held.load_sem.at[4 * chips + 1]),
        pltpu.make_async_copy(layer_out, held.layer_out, held.load_sem.at[4 * chips + 2]),
    ]
    for copy in more:
        copy.start()
    text_load.start()
    ends.bias_up[...] = sums[7:8, : ends.bias_up.shape[1]]
    ends.bias_down[...] = sums[6:7, :]
    ends.gain[...] = sums[0:3, :]
    ends.shift[...] = sums[3:6, :]

    def total(q, j):
        span = pl.ds(j * cols, cols)
        whole = held.shares[q, 0, :, span].astype(FULL)
        for c in range(1, chips):
            whole = whole + held.shares[q, c, :, span].astype(FULL)
        return whole

    for q in range(4):
        for copy in loads[q]:
            copy.wait()
        for j in range(parts):
            whole = total(q, j)
            if q == 0:
                held.w_down[pl.ds(j * cols, cols), :] = whole.T
            elif q == 1:
                held.w_up[:, pl.ds(j * cols, cols)] = whole
            elif j == 0:
                (held.wo_cross if q == 2 else held.wo_self)[...] = whole.T
            elif q == 3:
                held.w_self[j - 1] = whole
            elif j == 1:
                held.wq[...] = whole
            else:
                held.wkv[j - 2] = whole
        if q == 0:
            put(held.w_down, ends.w_down)
        elif q == 1:
            put(held.w_up, ends.w_up)
        elif q == 2:
            put(held.wo_cross, ends.wo_cross)
            put(held.wq, ends.wq)
            put(held.wkv, ends.wkv)
        else:
            put(held.wo_self, ends.wo_self)
            put(held.w_self, ends.w_self)
    more[0].wait()
    put(held.token_grad, ends.token_grad)
    more[1].wait()
    put(held.layer_out, ends.layer_out)
    text_load.wait()
    held.text[...] = held.text_low[...].astype(FULL)
    put(held.text, ends.text_grad)
    for copy in puts:
        copy.wait()


def local(
    n_mp,
    n_dp,
    tokens,
    text,
    text_len,
    text_mask,
    cotangent,
    w_self,
    wo_self,
    wq_cross,
    wkv_cross,
    wo_cross,
    w_up,
    bias_up,
    w_down,
    bias_down,
    ln_gain,
    ln_bias,
):
    images, seq, width = tokens.shape
    text_rows = text.shape[1]
    cols = w_self.shape[2]
    hidden = w_up.shape[1]
    heads = cols // HEAD_DIM
    rows = images * seq
    chips = n_dp // 2
    block = width // n_dp
    tile = min(512, hidden, width)

    def out(*shape, kind=LOW):
        return jax.ShapeDtypeStruct(shape, kind)

    outs = Outputs(
        layer_out=out(rows, width),
        token_grad=out(rows, width, kind=FULL),
        text_sum=out(images * text_rows, width),
        shares=out(4, chips, block, hidden),
        sums_out=out(8, width, kind=FULL),
        norm1=out(rows, width),
        norm2=out(rows, width),
        norm3=out(rows, width),
        low1=out(rows, width),
        low2=out(rows, width),
        act_all=out(rows, hidden),
        pre_all=out(rows, hidden),
        after_self=out(rows, width, kind=FULL),
        after_cross=out(rows, width, kind=FULL),
        grad_rows=out(rows, width, kind=FULL),
        staged=out(4 * chips, block, hidden),
    )
    slots = 2 * images

    def buf(*shape, kind=LOW):
        return pltpu.VMEM(shape, kind)

    dma = pltpu.SemaphoreType.DMA
    scratch = Scratch(
        wide=buf(width, hidden),
        down=buf(hidden, width),
        kv_w=buf(width, 2 * cols),
        q_w=buf(width, cols),
        o_w=buf(cols, width),
        inbox=buf(slots, seq, width),
        outbox=buf(images, seq, width),
        part=buf(images, seq, width),
        proj=buf(images, seq, 3 * cols),
        mix1=buf(images, seq, cols),
        prob1=buf(images, heads, seq, seq),
        q2=buf(images, seq, cols),
        kv2=buf(images, text_rows, 2 * cols),
        mix2=buf(images, seq, cols),
        prob2=buf(images, heads, seq, text_rows),
        hid32=buf(seq, width, kind=FULL),
        grad32=buf(seq, width, kind=FULL),
        normed=buf(seq, width),
        rows16=buf(seq, width),
        d_pre=buf(seq, hidden),
        active=buf(seq, hidden),
        d_mix=buf(seq, cols),
        tile=buf(2 * block, hidden),
        tile_sum=buf(block, hidden),
        tile_in=buf(2, block, hidden),
        unit_cols=buf(3, rows, max(tile, 2 * block)),
        x_text=buf(images * text_rows, 2 * block),
        sums=buf(8, width, kind=FULL),
        sums_in=buf(n_dp, 8, width, kind=FULL),
        send_sem=dma((images, PIECES)),
        out_sem=dma((images, PIECES)),
        in_sem=dma((slots, PIECES)),
        pass_sem=dma((slots, PIECES)),
        weight_sem=dma((3 + width // cols + 5,)),
        load_sem=dma((3,)),
        store_sem=dma((4,)),
        unit_sem=dma((6,)),
        core_send=dma((4 * chips,)),
        core_recv=dma((4 * chips,)),
        chip_send=dma((4 * chips,)),
        chip_recv=dma((4, chips)),
        sum_send=dma((n_dp,)),
        sum_recv=dma((n_dp,)),
    )
    vmem = pl.BlockSpec(memory_space=pltpu.VMEM)
    anywhere = pl.BlockSpec(memory_space=pl.ANY)
    sizes = (n_mp, n_dp, images, seq, width, text_rows, cols, hidden)
    results = pl.pallas_call(
        functools.partial(layer_kernel, sizes),
        out_shape=tuple(outs),
        in_specs=list(
            Inputs(*[anywhere] * len(Inputs._fields))._replace(
                length=vmem, kept=vmem, bias_up=vmem, bias_down=vmem, gain=vmem, shift=vmem
            )
        ),
        out_specs=tuple(Outputs(*[anywhere] * len(outs))._replace(sums_out=vmem)),
        scratch_shapes=list(scratch),
        compiler_params=pltpu.CompilerParams(
            collective_id=0, has_side_effects=True, vmem_limit_bytes=VMEM_LIMIT
        ),
        name="layer",
    )(
        tokens.reshape(rows, width),
        text.reshape(images * text_rows, width),
        text_len.reshape(1, images),
        text_mask,
        cotangent.reshape(rows, width),
        w_self,
        wo_self,
        wq_cross,
        wkv_cross,
        wo_cross,
        w_up,
        bias_up.reshape(1, hidden),
        w_down,
        bias_down.reshape(1, width),
        ln_gain,
        ln_bias,
    )
    got = Outputs(*results)
    shapes = Ends(
        layer_out=out(rows, width),
        token_grad=out(rows, width, kind=FULL),
        text_grad=out(images * text_rows, width, kind=FULL),
        w_self=out(3, block, cols, kind=FULL),
        wo_self=out(cols, block, kind=FULL),
        wq=out(block, cols, kind=FULL),
        wkv=out(2, block, cols, kind=FULL),
        wo_cross=out(cols, block, kind=FULL),
        w_up=out(block, hidden, kind=FULL),
        bias_up=out(1, hidden, kind=FULL),
        w_down=out(hidden, block, kind=FULL),
        bias_down=out(1, width, kind=FULL),
        gain=out(3, width, kind=FULL),
        shift=out(3, width, kind=FULL),
    )
    staging = Held(
        shares=buf(4, chips, block, hidden),
        text_low=buf(images * text_rows, width),
        text=buf(images * text_rows, width, kind=FULL),
        token_grad=buf(rows, width, kind=FULL),
        layer_out=buf(rows, width),
        w_self=buf(3, block, cols, kind=FULL),
        wo_self=buf(cols, block, kind=FULL),
        wq=buf(block, cols, kind=FULL),
        wkv=buf(2, block, cols, kind=FULL),
        wo_cross=buf(cols, block, kind=FULL),
        w_up=buf(block, hidden, kind=FULL),
        w_down=buf(hidden, block, kind=FULL),
        load_sem=dma((4 * chips + 3,)),
        put_sem=dma((10,)),
    )
    ends = Ends(
        *pl.pallas_call(
            functools.partial(closing_kernel, chips, cols),
            out_shape=tuple(shapes),
            in_specs=[anywhere] * 4 + [vmem],
            out_specs=tuple(
                Ends(*[anywhere] * len(shapes))._replace(
                    bias_up=vmem, bias_down=vmem, gain=vmem, shift=vmem
                )
            ),
            scratch_shapes=list(staging),
            compiler_params=pltpu.CompilerParams(vmem_limit_bytes=VMEM_LIMIT),
            name="closing",
        )(got.shares, got.token_grad, got.layer_out, got.text_sum, got.sums_out)
    )
    return (
        ends.layer_out.reshape(images, seq, width),
        ends.token_grad.reshape(images, seq, width),
        ends.text_grad.reshape(images, text_rows, width),
        ends.w_self,
        ends.wo_self,
        ends.wq,
        ends.wkv,
        ends.wo_cross,
        ends.w_up,
        ends.bias_up.reshape(hidden),
        ends.w_down,
        ends.bias_down.reshape(width),
        ends.gain,
        ends.shift,
    )


def solution(mesh):
    placed = (
        P("dp", None, None),
        P("dp", None, None),
        P("dp"),
        P("dp", None),
        P("dp", None, None),
        P(None, None, "mp"),
        P("mp", None),
        P(None, "mp"),
        P(None, None, "mp"),
        P("mp", None),
        P(None, "mp"),
        P("mp"),
        P("mp", None),
        P(),
        P(),
        P(),
    )
    return jax.shard_map(
        functools.partial(local, mesh.shape["mp"], mesh.shape["dp"]),
        mesh=mesh,
        in_specs=placed,
        out_specs=(
            P("dp", None, None),
            P("dp", None, None),
            P("dp", None, None),
            P(None, "dp", "mp"),
            P("mp", "dp"),
            P("dp", "mp"),
            P(None, "dp", "mp"),
            P("mp", "dp"),
            P("dp", "mp"),
            P("mp"),
            P("mp", "dp"),
            P(),
            P(),
            P(),
        ),
        check_vma=False,
    )
```
